128 devices in a mesh: rep: 8 (over y, core), tp: 16 (over x, z).
Axes of the slice: x: 4, y: 4, z: 4, core: 2. Of those that a mesh axis runs over, the one named last changes fastest.
Arguments:
- learner_rows: bfloat16 [18432, 8192], P(('rep', 'tp'))
- learner_slot: int32 [18432], replicated, may hold values from 0 to 18431, as said below
- query_order: int32 [128], replicated, may hold values from 0 to 127, each once
- kv_order: int32 [16], replicated, may hold values from 0 to 7, as said below
- tokens: bfloat16 [8192, 8192], P(('rep', 'tp')), may hold values from -6 to 6
- positions: int32 [8192], P('rep'), may hold values from 0 to 5118, as said below
Outputs:
- refit_weight: bfloat16 [20480, 8192], P('tp')
- qkv_rope: bfloat16 [8192, 20480], P('rep', 'tp')
The draws below stay inside these ranges and needn't reach their ends.
Inputs may be any that keep to these rules, and one draw needn't show every extreme that they name: learner_slot is a permutation of the 18432 slots; the learner device with index d (rep major) holds slots d * 144 to (d + 1) * 144 - 1, and within that block the slots h * 1 to (h + 1) - 1 hold rows of joined head block h, that is of rows h * 128 to (h + 1) * 128 - 1. `kv_order`: each key-value head appears exactly 16/8 times. `positions`: within each replica's block of 1024 tokens a position is one more than the one before, or 0 where a document begins; the first token of a block has a position below 4096; one replica's block begins at 4095 and has no document start, and the next replica's block has a document start at token 512.
All inputs are finite; a program needn't handle non-finite values.
Results may differ from the reference program's by a relative error of at most 0.0049.
Values may be sent and summed in bfloat16 or wider, within the bound.
A program may use at most 256 MiB of HBM per device.

```python
import math
import jax
import jax.numpy as jnp
from jax import lax

DW = 8192
HD = 128
QH = 128
KVH = 8
HEADS = 144
JOINED = 18432
QH_TP = 8
GROUP = 10
ROWS_TP = 1280
SPAN = 1024
N_REP = 8
N_TP = 16


def draw_learner_rows(key, part):
    key = jax.random.fold_in(key, 11)
    base_key, row_key, col_key = jax.random.split(key, 3)
    row_factor = jnp.exp(jax.random.uniform(row_key, (JOINED, 1), jnp.float32, math.log(0.3), math.log(3.0)))
    col_factor = jnp.exp(jax.random.uniform(col_key, (1, DW), jnp.float32, math.log(0.3), math.log(3.0)))
    base = jax.random.normal(base_key, (JOINED, DW), jnp.float32)
    return (base * row_factor * col_factor * DW ** (-0.5)).astype(jnp.bfloat16)


def draw_learner_slot(key, part):
    key = jax.random.fold_in(key, 23)
    per_head = HD // (N_REP * N_TP)
    head_keys = jax.random.split(key, HEADS)
    orders = jax.vmap(lambda one_key: jax.random.permutation(one_key, HD))(head_keys).astype(jnp.int32)
    device_ids = orders // per_head
    within_head = orders % per_head
    head_ids = jnp.arange(HEADS, dtype=jnp.int32)[:, None]
    slot_ids = device_ids * (HEADS * per_head) + head_ids * per_head + within_head
    return slot_ids.reshape(-1).astype(jnp.int32)


def draw_kv_order(key, part):
    key = jax.random.fold_in(key, 37)
    return (jax.random.permutation(key, N_TP).astype(jnp.int32) % KVH).astype(jnp.int32)


def draw_positions(key, part):
    key = jax.random.fold_in(key, 41)
    flag_key, offset_key, pick_key = jax.random.split(key, 3)
    index_rows = jnp.broadcast_to(jnp.arange(SPAN, dtype=jnp.int32)[None, :], (N_REP, SPAN))
    replica_ids = jnp.broadcast_to(jnp.arange(N_REP, dtype=jnp.int32)[:, None], (N_REP, SPAN))
    chosen = jax.random.randint(pick_key, (), 0, N_REP).astype(jnp.int32)
    follower = (chosen + 1) % N_REP
    random_starts = jax.random.randint(flag_key, (N_REP, SPAN), 0, 384) == 0
    forced_start = (replica_ids == follower) & (index_rows == SPAN // 2)
    starts = random_starts & (replica_ids != chosen) | forced_start | (index_rows == 0)
    last_start = lax.cummax(jnp.where(starts, index_rows, 0), axis=1)
    offsets = jax.random.randint(offset_key, (N_REP, 1), 0, 4096).astype(jnp.int32)
    offsets = jnp.where(jnp.arange(N_REP, dtype=jnp.int32)[:, None] == chosen, 4095, offsets).astype(jnp.int32)
    place_ids = index_rows - last_start + jnp.where(last_start == 0, offsets, 0)
    return place_ids.reshape(-1).astype(jnp.int32)


def levels(rng, extent, shards, smallest, high):
    def one(position, parts):
        steps = jax.random.uniform(jax.random.fold_in(jax.random.fold_in(rng, 6), position), (parts,), jnp.float32, smallest / len(shards), high / len(shards))
        return jnp.repeat(jnp.exp(steps), extent[position] // parts).reshape((-1,) + (1,) * (len(extent) - position - 1))

    factor_of = one(*shards[0])
    for cut in shards[1:]:
        factor_of = factor_of * one(*cut)
    return factor_of


def normal_values(key, shape, deviation, most, pieces=(), kind=jnp.bfloat16):
    values = deviation * jax.random.normal(key, shape, jnp.float32)
    if pieces:
        values = values * levels(key, shape, pieces, -0.22, 0.18)
    return jnp.clip(values, -most, most).astype(kind)


def setup_inputs(seed: int = 0) -> dict:
    splits = jax.random.split(jax.random.key(seed), 7)
    return {
        "learner_rows": draw_learner_rows(jax.random.fold_in(splits[6], 71), 0),
        "learner_slot": draw_learner_slot(jax.random.fold_in(splits[6], 71), 0),
        "query_order": jax.random.permutation(splits[2], QH).astype(jnp.int32),
        "kv_order": draw_kv_order(jax.random.fold_in(splits[6], 71), 0),
        "tokens": normal_values(splits[4], (N_REP * SPAN, DW), 1.0, 6.0, ((0, 128),)),
        "positions": draw_positions(jax.random.fold_in(splits[6], 71), 0),
    }


epsilon = 1e-6
rope_base = 500000.0


def rotate(values, place_ids, head_total, group_size):
    row_total = values.shape[0]
    half_dim = HD // 2
    frequency = jnp.exp(jnp.arange(half_dim, dtype=jnp.float32) * (-2.0 * math.log(rope_base) / HD))
    angles = place_ids.astype(jnp.float32)[:, None] * frequency[None, :]
    cosines = jnp.cos(angles)[:, None, :]
    sines = jnp.sin(angles)[:, None, :]
    shaped = values.reshape(row_total, head_total, HD)
    lower_half = shaped[:, :, :half_dim]
    upper_half = shaped[:, :, half_dim:]
    turned = jnp.concatenate([lower_half * cosines - upper_half * sines, upper_half * cosines + lower_half * sines], axis=2)
    keep_value = (jnp.arange(head_total) % group_size == group_size - 1)[None, :, None]
    return jnp.where(keep_value, shaped, turned).reshape(row_total, head_total * HD)


def reference(learner_rows, learner_slot, query_order, kv_order, tokens, positions):
    largest = jnp.max(jnp.abs(learner_rows), axis=1).astype(jnp.float32)
    row_scale = (largest + epsilon).astype(jnp.bfloat16)
    quantized = (learner_rows.astype(jnp.float32) / row_scale.astype(jnp.float32)[:, None]).astype(jnp.bfloat16)
    head_table = jnp.concatenate([query_order.reshape(N_TP, QH_TP), QH + kv_order[:, None], QH + KVH + kv_order[:, None]], axis=1)
    joined_ids = (head_table[:, :, None] * HD + jnp.arange(HD, dtype=jnp.int32)[None, None, :]).reshape(-1)
    slot_ids = jnp.take(learner_slot, joined_ids)
    refit_weight = jnp.take(quantized, slot_ids, axis=0)
    column_scale = jnp.take(row_scale, slot_ids).astype(jnp.float32)
    head_total = N_TP * GROUP

    def one_replica(block):
        token_rows, place_ids = block
        product = jnp.dot(token_rows, refit_weight.T, preferred_element_type=jnp.float32)
        return rotate(product * column_scale[None, :], place_ids, head_total, GROUP).astype(jnp.bfloat16)

    qkv_rope = lax.map(one_replica, (tokens.reshape(N_REP, SPAN, DW), positions.reshape(N_REP, SPAN)))
    return refit_weight, qkv_rope.reshape(N_REP * SPAN, N_TP * ROWS_TP)
```

```python
import functools
import math

import jax
import jax.numpy as jnp
from jax import lax
from jax.experimental import pallas as pl
from jax.experimental.pallas import tpu as pltpu
from jax.sharding import PartitionSpec as P

HD = 128
QH = 128
KVH = 8
HEADS = 144
GROUP = 10
DW = 8192
SPAN = 1024
ROWS = 64
PAIRS = 5
SUB = 1024
QS = DW // SUB
HALF = DW // 2
WIDE = PAIRS * SUB + 128
SLOTS = 2048

epsilon = 1e-06
rope_base = 500000.0
MESH = pl.DeviceIdType.MESH


def columns_of(pair):
    if pair == 0:
        return pl.ds(0, SUB + 128)
    return pl.ds(128 + pair * SUB, SUB)


def data_of(pair):
    return pl.ds(128 + pair * SUB, SUB)


def exchange(
    tokens,
    learner,
    slots,
    query_row,
    kv_row,
    query_s,
    kv_s,
    all_tokens,
    placed,
    scales,
    rows,
    stacked,
    sending,
    slab,
    stage,
    turned,
    t_send,
    t_recv,
    w_send,
    w_recv,
    a_send,
    a_recv,
    c_recv,
    l_sem,
    s_sem,
):
    rep = lax.axis_index("rep")
    tp = lax.axis_index("tp")
    y, core = rep // 2, rep % 2
    x, z = tp // 4, tp % 4

    def place_of(dx, dz):
        return lax.rem(x + dx + 4, 4) * 4 + lax.rem(z + dz + 4, 4)

    def rep_of(dy):
        return lax.rem(y + dy + 4, 4) * 2 + core

    twin = y * 2 + 1 - core

    load_rows = pltpu.make_async_copy(learner, rows, l_sem.at[0])
    load_rows.start()
    own_copy = pltpu.make_async_copy(tokens, all_tokens.at[tp], l_sem.at[1])
    own_copy.start()

    barrier = pltpu.get_barrier_semaphore()
    offsets = [(dx, dz) for dx in (1, 3, 0, 2) for dz in (1, 3, 0, 2) if (dx, dz) != (0, 0)]
    for dx, dz in offsets:
        pl.semaphore_signal(barrier, inc=1, device_id=(rep, place_of(dx, dz)), device_id_type=MESH)
    for other in (rep_of(1), rep_of(3), twin):
        pl.semaphore_signal(barrier, inc=1, device_id=(other, tp), device_id_type=MESH)
    pl.semaphore_wait(barrier, len(offsets) + 3)

    def along(half, phase, step):
        return place_of(step, 0) if (half == 0) == (phase == 0) else place_of(0, step)

    def block_at(half, first, second):
        return place_of(first, second) if half == 0 else place_of(second, first)

    def piece(ref, half, low, count):
        return ref.at[pl.ds(low, count), pl.ds(half * HALF, HALF)]

    started = []

    def token_copy(half, number, block, low, count, phase, step, own=False):
        k = half * 20 + number
        source = piece(tokens, half, low, count) if own else piece(all_tokens.at[block], half, low, count)
        copy = pltpu.make_async_remote_copy(
            src_ref=source,
            dst_ref=piece(all_tokens.at[block], half, low, count),
            send_sem=t_send.at[k],
            recv_sem=t_recv.at[k],
            device_id=(rep, along(half, phase, step)),
            device_id_type=MESH,
        )
        copy.start()
        started.append(copy)

    def token_wait(half, number, block, low, count):
        k = half * 20 + number
        here = piece(all_tokens.at[block], half, low, count)
        pltpu.make_async_copy(here, here, t_recv.at[k]).wait()

    def first_sends():
        for half in (0, 1):
            token_copy(half, 0, tp, 0, ROWS, 0, 1, own=True)
            token_copy(half, 1, tp, 0, ROWS, 0, -1, own=True)

    order = (0, -1, 1, 2)

    def second_sends(half, k):
        block = block_at(half, order[k], 0)
        token_copy(half, 4 + 4 * k, block, 0, ROWS, 1, 1, own=k == 0)
        token_copy(half, 5 + 4 * k, block, 0, ROWS, 1, -1, own=k == 0)

    def token_step(number):
        for half in (0, 1):
            if number == 0:
                second_sends(half, 0)
            elif number == 1:
                block = block_at(half, -1, 0)
                token_wait(half, 0, block, 0, ROWS)
                token_copy(half, 2, block, 0, ROWS // 2, 0, 1)
                second_sends(half, 1)
            elif number == 2:
                block = block_at(half, 1, 0)
                token_wait(half, 1, block, 0, ROWS)
                token_copy(half, 3, block, ROWS // 2, ROWS // 2, 0, -1)
                second_sends(half, 2)
            elif number == 3:
                block = block_at(half, 2, 0)
                token_wait(half, 2, block, 0, ROWS // 2)
                token_wait(half, 3, block, ROWS // 2, ROWS // 2)
                second_sends(half, 3)
            elif number < 8:
                k = number - 4
                block = block_at(half, order[k], -1)
                token_wait(half, 4 + 4 * k, block, 0, ROWS)
                token_copy(half, 6 + 4 * k, block, 0, ROWS // 2, 1, 1)
                block = block_at(half, order[k], 1)
                token_wait(half, 5 + 4 * k, block, 0, ROWS)
                token_copy(half, 7 + 4 * k, block, ROWS // 2, ROWS // 2, 1, -1)
            else:
                k = number - 8
                block = block_at(half, order[k], 2)
                token_wait(half, 6 + 4 * k, block, 0, ROWS // 2)
                token_wait(half, 7 + 4 * k, block, ROWS // 2, ROWS // 2)

    def block_rows(core_, y_, low=0, count=256):
        return pl.ds(pl.multiple_of((core_ * 4 + y_) * 256, 256) + low, count)

    mine = block_rows(core, y)

    def weight_copy(pair, number, rows_, recv, device):
        k = pair * 8 + number
        here = slab.at[rows_, columns_of(pair)]
        copy = pltpu.make_async_remote_copy(
            src_ref=here, dst_ref=here, send_sem=w_send.at[k], recv_sem=recv, device_id=device, device_id_type=MESH
        )
        copy.start()
        started.append(copy)

    def weight_wait(pair, rows_, sem):
        here = slab.at[rows_, columns_of(pair)]
        pltpu.make_async_copy(here, here, sem).wait()

    def scatter(pair):
        for dx, dz in offsets:
            to = place_of(dx, dz)
            pltpu.make_async_remote_copy(
                src_ref=sending.at[pl.ds(pl.multiple_of(to * 16, 16), 16), columns_of(pair)],
                dst_ref=slab.at[
                    pl.ds(pl.multiple_of((core * 4 + y) * 256 + tp * 16, 16), 16), columns_of(pair)
                ],
                send_sem=a_send.at[pair],
                recv_sem=a_recv.at[pair],
                device_id=(rep, to),
                device_id_type=MESH,
            ).start()
        pltpu.make_async_copy(
            sending.at[pl.ds(pl.multiple_of(tp * 16, 16), 16), columns_of(pair)],
            slab.at[pl.ds(pl.multiple_of((core * 4 + y) * 256 + tp * 16, 16), 16), columns_of(pair)],
            s_sem.at[pair],
        ).start()

    ym, yp, y2 = lax.rem(y + 3, 4), lax.rem(y + 1, 4), lax.rem(y + 2, 4)
    up, down, across = (rep_of(1), tp), (rep_of(-1), tp), (twin, tp)

    def gathered(pair):
        fifteen = slab.at[block_rows(core, y, 0, 240), columns_of(pair)]
        pltpu.make_async_copy(fifteen, fifteen, a_recv.at[pair]).wait()
        one = slab.at[block_rows(core, y, 0, 16), columns_of(pair)]
        pltpu.make_async_copy(one, one, s_sem.at[pair]).wait()
        weight_copy(pair, 0, mine, w_recv.at[pair * 4], up)
        weight_copy(pair, 1, mine, w_recv.at[pair * 4 + 1], down)
        weight_copy(pair, 4, mine, c_recv.at[pair], across)

    def relayed(pair):
        weight_wait(pair, block_rows(core, ym), w_recv.at[pair * 4])
        weight_copy(pair, 2, block_rows(core, ym, 0, 128), w_recv.at[pair * 4 + 2], up)
        weight_copy(pair, 5, block_rows(core, ym), c_recv.at[pair], across)
        weight_wait(pair, block_rows(core, yp), w_recv.at[pair * 4 + 1])
        weight_copy(pair, 3, block_rows(core, yp, 128, 128), w_recv.at[pair * 4 + 3], down)
        weight_copy(pair, 6, block_rows(core, yp), c_recv.at[pair], across)

    def opposite(pair):
        weight_wait(pair, block_rows(core, y2, 0, 128), w_recv.at[pair * 4 + 2])
        weight_wait(pair, block_rows(core, y2, 128, 128), w_recv.at[pair * 4 + 3])
        weight_copy(pair, 7, block_rows(core, y2), c_recv.at[pair], across)

    def crossed(pair):
        weight_wait(pair, pl.ds(pl.multiple_of((1 - core) * 1024, 1024), 1024), c_recv.at[pair])

    def place(pair):
        buffer = pair % 2
        if pair >= 2:
            stored(pair - 2).wait()

        def columns(q, carry):
            lane = lax.broadcasted_iota(jnp.int32, (HD, SLOTS), 1)
            parts = []
            for i in (0, 1):
                want = turned[:, pl.ds(2 * pair + i, 1)] + (2 * q + i)
                parts.append(jnp.where(lane == want, 1.0, 0.0).astype(jnp.bfloat16))
            picker = jnp.concatenate(parts, axis=0)
            stage[buffer, :, pl.ds(pl.multiple_of(q * SUB, SUB), SUB)] = jnp.dot(
                picker, slab[:, data_of(pair)], preferred_element_type=jnp.float32
            ).astype(jnp.bfloat16)

            @pl.when(q == 0)
            def _():
                scales[pl.ds(pair * 256, 256), :] = jnp.dot(
                    picker, slab[:, pl.ds(0, 128)], preferred_element_type=jnp.float32
                )

            return carry

        lax.fori_loop(0, QS, columns, 0)
        stored(pair).start()

    def stored(pair):
        return pltpu.make_async_copy(
            stage.at[pair % 2], placed.at[pl.ds(pair * 256, 256)], l_sem.at[2 + pair % 2]
        )

    first_sends()
    load_rows.wait()

    largest = jnp.zeros((HEADS, 1), jnp.float32)
    for q in range(QS):
        part = jnp.abs(rows[:, pl.ds(q * SUB, SUB)].astype(jnp.float32))
        largest = jnp.maximum(largest, jnp.max(part, axis=1, keepdims=True))
    row_scale = (largest + epsilon).astype(jnp.bfloat16)
    scale = row_scale.astype(jnp.float32)
    for q in range(QS):
        stacked[pl.ds(q * HEADS, HEADS), :] = (
            rows[:, pl.ds(q * SUB, SUB)].astype(jnp.float32) / scale
        ).astype(jnp.bfloat16)
    wide_scale = jnp.broadcast_to(scale, (HEADS, 128)).astype(jnp.bfloat16)

    def head_column(pair):
        row = lax.broadcasted_iota(jnp.int32, (256, 128), 0)
        lane = lax.broadcasted_iota(jnp.int32, (256, 128), 1)
        u, i = row // 16, row % 2
        if pair < 4:
            chosen = jnp.where(lane == u * 8 + 2 * pair + i, query_row[0:1, :], 0)
            return jnp.sum(chosen.astype(jnp.float32), axis=1, keepdims=True).astype(jnp.int32)
        chosen = jnp.where(lane == u, kv_row[0:1, :] + QH + KVH * i, 0)
        return jnp.sum(chosen.astype(jnp.float32), axis=1, keepdims=True).astype(jnp.int32)

    heads = [head_column(pair) for pair in range(PAIRS)]
    tile = jnp.zeros((256, 128), jnp.float32)
    lane = lax.broadcasted_iota(jnp.int32, (256, HEADS), 1)
    lane128 = lax.broadcasted_iota(jnp.int32, (256, 128), 1)
    for pair in range(PAIRS):
        pick = jnp.where(lane == heads[pair], 1.0, 0.0).astype(jnp.bfloat16)
        got = jnp.dot(pick, wide_scale, preferred_element_type=jnp.float32)
        tile = jnp.where(lane128 == pair, got, tile)
    sending[:, pl.ds(0, 128)] = tile.astype(jnp.bfloat16)

    def prepare(pair):
        piece_of = (lax.broadcasted_iota(jnp.int32, (256, 1), 0) // 2) % QS
        want = heads[pair] + piece_of * HEADS
        lanes = lax.broadcasted_iota(jnp.int32, (256, QS * HEADS), 1)
        pick = jnp.where(lanes == want, 1.0, 0.0).astype(jnp.bfloat16)
        sending[:, data_of(pair)] = jnp.dot(
            pick, stacked[...], preferred_element_type=jnp.float32
        ).astype(jnp.bfloat16)

    for pair in range(PAIRS):
        prepare(pair)
        scatter(pair)
        if pair == 1:
            token_step(0)

    turned[...] = jnp.zeros_like(turned)
    for i in range(GROUP):
        if i < 8:
            head = query_s[tp * 8 + i]
        else:
            head = kv_s[tp] + QH + KVH * (i - 8)
        slot = slots[pl.ds(head, 1), :]
        source = ((slot.astype(jnp.float32) + 0.5) * (1.0 / HEADS)).astype(jnp.int32)
        at = ((source // 16) % 2 * 4 + source // 32) * 256 + (source % 16) * 16
        turned[i : i + 1, :] = at
    turned[...] = jnp.transpose(turned[...].astype(jnp.float32)).astype(jnp.int32)

    gathered(0)
    token_step(1)
    gathered(1)
    token_step(2)
    relayed(0)
    gathered(2)
    token_step(3)
    opposite(0)
    relayed(1)
    gathered(3)
    crossed(0)
    place(0)
    token_step(4)
    opposite(1)
    relayed(2)
    gathered(4)
    crossed(1)
    place(1)
    token_step(5)
    opposite(2)
    relayed(3)
    crossed(2)
    place(2)
    token_step(6)
    token_step(8)
    opposite(3)
    relayed(4)
    crossed(3)
    place(3)
    token_step(7)
    token_step(9)
    opposite(4)
    crossed(4)
    place(4)
    token_step(10)
    token_step(11)

    own_copy.wait()
    stored(3).wait()
    stored(4).wait()
    for copy in started:
        copy.wait_send()
    for pair in range(PAIRS):
        fifteen = sending.at[pl.ds(0, 240), columns_of(pair)]
        pltpu.make_async_copy(fifteen, fifteen, a_send.at[pair]).wait()


def project(tokens, weight, scales, cosines, sines, refit, out, held, t_sem, r_sem):
    pair = pl.program_id(0)

    def load(k):
        return pltpu.make_async_copy(
            tokens.at[pl.ds(k * 256, 256)], held.at[pl.ds(k * 256, 256)], t_sem.at[k]
        )

    @pl.when(pair == 0)
    def _():
        for k in range(4):
            load(k).start()

    keep = pltpu.make_async_copy(weight, refit.at[pl.ds(pl.multiple_of(pair * 256, 256), 256)], r_sem)
    keep.start()

    lane = lax.broadcasted_iota(jnp.int32, (8, 128), 1)
    chosen = jnp.where(lane == pair, 1.0, 0.0).astype(jnp.bfloat16)
    column_scale = lax.dot_general(
        chosen,
        scales[...].astype(jnp.bfloat16),
        (((1,), (1,)), ((), ())),
        preferred_element_type=jnp.float32,
    )[0:1, :]

    for k in range(4):

        @pl.when(pair == 0)
        def _():
            load(k).wait()

        rows = pl.ds(k * 256, 256)
        product = lax.dot_general(
            held[rows, :], weight[...], (((1,), (1,)), ((), ())), preferred_element_type=jnp.float32
        )
        product = product * column_scale
        for i in (0, 1):
            part = product[:, i * HD : (i + 1) * HD]
            turn = part * cosines[rows, :] + pltpu.roll(part, HD // 2, 1) * sines[rows, :]
            if i == 1:
                turn = jnp.where(pair == PAIRS - 1, part, turn)
            out[rows, pl.ds(i * HD, HD)] = turn.astype(jnp.bfloat16)
    keep.wait()


def per_device(learner_rows, learner_slot, query_order, kv_order, tokens, positions):
    any_space = pl.BlockSpec(memory_space=pl.ANY)
    vmem = pl.BlockSpec(memory_space=pltpu.VMEM)
    smem = pl.BlockSpec(memory_space=pltpu.SMEM)
    dma = pltpu.SemaphoreType.DMA
    all_tokens, placed, scales = pl.pallas_call(
        exchange,
        out_shape=(
            jax.ShapeDtypeStruct((16, ROWS, DW), jnp.bfloat16),
            jax.ShapeDtypeStruct((GROUP * HD, DW), jnp.bfloat16),
            jax.ShapeDtypeStruct((GROUP * HD, 128), jnp.float32),
        ),
        in_specs=[any_space, any_space, vmem, vmem, vmem, smem, smem],
        out_specs=(any_space, any_space, vmem),
        scratch_shapes=[
            pltpu.VMEM((HEADS, DW), jnp.bfloat16),
            pltpu.VMEM((QS * HEADS, SUB), jnp.bfloat16),
            pltpu.VMEM((256, WIDE), jnp.bfloat16),
            pltpu.VMEM((SLOTS, WIDE), jnp.bfloat16),
            pltpu.VMEM((2, 256, DW), jnp.bfloat16),
            pltpu.VMEM((HD, HD), jnp.int32),
            dma((40,)),
            dma((40,)),
            dma((40,)),
            dma((20,)),
            dma((PAIRS,)),
            dma((PAIRS,)),
            dma((PAIRS,)),
            dma((4,)),
            dma((PAIRS,)),
        ],
        compiler_params=pltpu.CompilerParams(
            collective_id=0, has_side_effects=True, vmem_limit_bytes=56 * 2**20
        ),
    )(
        tokens,
        learner_rows,
        learner_slot.reshape(HEADS, HD),
        query_order.reshape(1, QH),
        jnp.pad(kv_order, (0, 128 - kv_order.shape[0])).reshape(1, 128),
        query_order,
        kv_order,
    )

    half = HD // 2
    frequency = jnp.exp(jnp.arange(half, dtype=jnp.float32) * (-2.0 * math.log(rope_base) / HD))
    angles = positions.astype(jnp.float32)[:, None] * frequency[None, :]
    cosines, sines = jnp.cos(angles), jnp.sin(angles)
    cosines = jnp.concatenate([cosines, cosines], axis=1)
    sines = jnp.concatenate([-sines, sines], axis=1)

    return pl.pallas_call(
        project,
        grid=(PAIRS,),
        out_shape=(
            jax.ShapeDtypeStruct((GROUP * HD, DW), jnp.bfloat16),
            jax.ShapeDtypeStruct((SPAN, GROUP * HD), jnp.bfloat16),
        ),
        in_specs=[
            any_space,
            pl.BlockSpec((256, DW), lambda p: (p, 0)),
            pl.BlockSpec((256, 128), lambda p: (p, 0)),
            pl.BlockSpec((SPAN, HD), lambda p: (0, 0)),
            pl.BlockSpec((SPAN, HD), lambda p: (0, 0)),
        ],
        out_specs=(any_space, pl.BlockSpec((SPAN, 256), lambda p: (0, p))),
        scratch_shapes=[pltpu.VMEM((SPAN, DW), jnp.bfloat16), dma((4,)), dma],
        compiler_params=pltpu.CompilerParams(vmem_limit_bytes=56 * 2**20),
    )(all_tokens.reshape(SPAN, DW), placed, scales, cosines, sines)


def solution(mesh):
    in_specs = (P(("rep", "tp"), None), P(), P(), P(), P(("rep", "tp"), None), P("rep"))
    out_specs = (P("tp", None), P("rep", "tp"))
    return jax.shard_map(
        per_device, mesh=mesh, in_specs=in_specs, out_specs=out_specs, check_vma=False
    )
```

```python
import functools
import math

import jax
import jax.numpy as jnp
from jax import lax
from jax.experimental import pallas as pl
from jax.experimental.pallas import tpu as pltpu
from jax.sharding import PartitionSpec as P

HD = 128
QH = 128
KVH = 8
HEADS = 144
GROUP = 10
DW = 8192
SPAN = 1024
ROWS = 64
PAIRS = 5
SUB = 1024
QS = DW // SUB
HALF = DW // 2
WIDE = PAIRS * SUB + 128
SCALES = PAIRS * SUB
SLOTS = 2048

epsilon = 1e-06
rope_base = 500000.0
MESH = pl.DeviceIdType.MESH


def columns_of(pair):
    return pl.ds(pair * SUB, SUB + 128 if pair == PAIRS - 1 else SUB)


def data_of(pair):
    return pl.ds(pair * SUB, SUB)


def exchange(
    tokens,
    learner,
    slots,
    query_row,
    kv_row,
    query_s,
    kv_s,
    position_rows,
    frequency,
    all_tokens,
    placed,
    scales,
    cosines,
    sines,
    rows,
    stacked,
    sending,
    arrived,
    slab,
    stage,
    turned,
    t_send,
    t_recv,
    w_send,
    w_recv,
    a_send,
    a_recv,
    c_recv,
    l_sem,
    s_sem,
):
    rep = lax.axis_index("rep")
    tp = lax.axis_index("tp")
    y, core = rep // 2, rep % 2
    x, z = tp // 4, tp % 4

    def place_of(dx, dz):
        return lax.rem(x + dx + 4, 4) * 4 + lax.rem(z + dz + 4, 4)

    def rep_of(dy):
        return lax.rem(y + dy + 4, 4) * 2 + core

    twin = y * 2 + 1 - core

    load_rows = pltpu.make_async_copy(learner, rows, l_sem.at[0])
    load_rows.start()
    own_copy = pltpu.make_async_copy(tokens, all_tokens.at[tp], l_sem.at[1])
    own_copy.start()

    barrier = pltpu.get_barrier_semaphore()
    offsets = [(dx, dz) for dx in (1, 3, 0, 2) for dz in (1, 3, 0, 2) if (dx, dz) != (0, 0)]
    for dx, dz in offsets:
        pl.semaphore_signal(barrier, inc=1, device_id=(rep, place_of(dx, dz)), device_id_type=MESH)
    for other in (rep_of(1), rep_of(3), twin):
        pl.semaphore_signal(barrier, inc=1, device_id=(other, tp), device_id_type=MESH)
    pl.semaphore_wait(barrier, len(offsets) + 3)

    def along(half, phase, step):
        return place_of(step, 0) if (half == 0) == (phase == 0) else place_of(0, step)

    def block_at(half, first, second):
        return place_of(first, second) if half == 0 else place_of(second, first)

    def piece(ref, half, low, count):
        return ref.at[pl.ds(low, count), pl.ds(half * HALF, HALF)]

    started = []

    def token_copy(half, number, block, low, count, phase, step, own=False):
        k = half * 20 + number
        source = piece(tokens, half, low, count) if own else piece(all_tokens.at[block], half, low, count)
        copy = pltpu.make_async_remote_copy(
            src_ref=source,
            dst_ref=piece(all_tokens.at[block], half, low, count),
            send_sem=t_send.at[k],
            recv_sem=t_recv.at[k],
            device_id=(rep, along(half, phase, step)),
            device_id_type=MESH,
        )
        copy.start()
        started.append(copy)

    def token_wait(half, number, block, low, count):
        k = half * 20 + number
        here = piece(all_tokens.at[block], half, low, count)
        pltpu.make_async_copy(here, here, t_recv.at[k]).wait()

    def first_sends():
        for half in (0, 1):
            token_copy(half, 0, tp, 0, ROWS, 0, 1, own=True)
            token_copy(half, 1, tp, 0, ROWS, 0, -1, own=True)

    order = (0, -1, 1, 2)

    def second_sends(half, k):
        block = block_at(half, order[k], 0)
        token_copy(half, 4 + 4 * k, block, 0, ROWS, 1, 1, own=k == 0)
        token_copy(half, 5 + 4 * k, block, 0, ROWS, 1, -1, own=k == 0)

    def token_step(number):
        for half in (0, 1):
            if number == 0:
                second_sends(half, 0)
            elif number == 1:
                block = block_at(half, -1, 0)
                token_wait(half, 0, block, 0, ROWS)
                token_copy(half, 2, block, 0, ROWS // 2, 0, 1)
                second_sends(half, 1)
            elif number == 2:
                block = block_at(half, 1, 0)
                token_wait(half, 1, block, 0, ROWS)
                token_copy(half, 3, block, ROWS // 2, ROWS // 2, 0, -1)
                second_sends(half, 2)
            elif number == 3:
                block = block_at(half, 2, 0)
                token_wait(half, 2, block, 0, ROWS // 2)
                token_wait(half, 3, block, ROWS // 2, ROWS // 2)
                second_sends(half, 3)
            elif number < 8:
                k = number - 4
                block = block_at(half, order[k], -1)
                token_wait(half, 4 + 4 * k, block, 0, ROWS)
                token_copy(half, 6 + 4 * k, block, 0, ROWS // 2, 1, 1)
                block = block_at(half, order[k], 1)
                token_wait(half, 5 + 4 * k, block, 0, ROWS)
                token_copy(half, 7 + 4 * k, block, ROWS // 2, ROWS // 2, 1, -1)
            else:
                k = number - 8
                block = block_at(half, order[k], 2)
                token_wait(half, 6 + 4 * k, block, 0, ROWS // 2)
                token_wait(half, 7 + 4 * k, block, ROWS // 2, ROWS // 2)

    def block_rows(core_, y_, low=0, count=256):
        return pl.ds(pl.multiple_of((core_ * 4 + y_) * 256, 256) + low, count)

    mine = block_rows(core, y)

    def weight_copy(pair, number, rows_, recv, device):
        k = pair * 8 + number
        here = slab.at[rows_, columns_of(pair)]
        copy = pltpu.make_async_remote_copy(
            src_ref=here, dst_ref=here, send_sem=w_send.at[k], recv_sem=recv, device_id=device, device_id_type=MESH
        )
        copy.start()
        started.append(copy)

    def weight_wait(pair, rows_, sem):
        here = slab.at[rows_, columns_of(pair)]
        pltpu.make_async_copy(here, here, sem).wait()

    def scatter(pair):
        for dx, dz in offsets:
            to = place_of(dx, dz)
            pltpu.make_async_remote_copy(
                src_ref=sending.at[pl.ds(pl.multiple_of(to * 16, 16), 16), columns_of(pair)],
                dst_ref=arrived.at[pl.ds(pl.multiple_of(tp * 16, 16), 16), columns_of(pair)],
                send_sem=a_send.at[pair],
                recv_sem=a_recv.at[pair],
                device_id=(rep, to),
                device_id_type=MESH,
            ).start()
        pltpu.make_async_copy(
            sending.at[pl.ds(pl.multiple_of(tp * 16, 16), 16), columns_of(pair)],
            arrived.at[pl.ds(pl.multiple_of(tp * 16, 16), 16), columns_of(pair)],
            s_sem.at[pair],
        ).start()

    ym, yp, y2 = lax.rem(y + 3, 4), lax.rem(y + 1, 4), lax.rem(y + 2, 4)
    up, down, across = (rep_of(1), tp), (rep_of(-1), tp), (twin, tp)

    def gathered(pair):
        fifteen = arrived.at[pl.ds(0, 240), columns_of(pair)]
        pltpu.make_async_copy(fifteen, fifteen, a_recv.at[pair]).wait()
        one = arrived.at[pl.ds(0, 16), columns_of(pair)]
        pltpu.make_async_copy(one, one, s_sem.at[pair]).wait()
        row = lax.broadcasted_iota(jnp.int32, (256, 256), 0)
        lane = lax.broadcasted_iota(jnp.int32, (256, 256), 1)
        swap = jnp.where(lane == (row % 16) * 16 + row // 16, 1.0, 0.0).astype(jnp.bfloat16)
        slab[mine, columns_of(pair)] = jnp.dot(
            swap, arrived[:, columns_of(pair)], preferred_element_type=jnp.float32
        ).astype(jnp.bfloat16)
        weight_copy(pair, 0, mine, w_recv.at[pair * 4], up)
        weight_copy(pair, 1, mine, w_recv.at[pair * 4 + 1], down)
        weight_copy(pair, 4, mine, c_recv.at[pair], across)

    def relayed(pair):
        weight_wait(pair, block_rows(core, ym), w_recv.at[pair * 4])
        weight_copy(pair, 2, block_rows(core, ym, 0, 128), w_recv.at[pair * 4 + 2], up)
        weight_copy(pair, 5, block_rows(core, ym), c_recv.at[pair], across)
        weight_wait(pair, block_rows(core, yp), w_recv.at[pair * 4 + 1])
        weight_copy(pair, 3, block_rows(core, yp, 128, 128), w_recv.at[pair * 4 + 3], down)
        weight_copy(pair, 6, block_rows(core, yp), c_recv.at[pair], across)

    def opposite(pair):
        weight_wait(pair, block_rows(core, y2, 0, 128), w_recv.at[pair * 4 + 2])
        weight_wait(pair, block_rows(core, y2, 128, 128), w_recv.at[pair * 4 + 3])
        weight_copy(pair, 7, block_rows(core, y2), c_recv.at[pair], across)

    def crossed(pair):
        weight_wait(pair, pl.ds(pl.multiple_of((1 - core) * 1024, 1024), 1024), c_recv.at[pair])

    def place(pair):
        buffer = pair % 2
        if pair >= 2:
            stored(pair - 2).wait()

        lane = lax.broadcasted_iota(jnp.int32, (HD, HD), 1)
        none = jnp.zeros((HD, HD), jnp.float32)
        first = jnp.where(lane == turned[:, 2 * pair : 2 * pair + 1], 1.0, 0.0)
        second = jnp.where(lane == turned[:, 2 * pair + 1 : 2 * pair + 2], 1.0, 0.0)
        picker = jnp.concatenate(
            [jnp.concatenate([first, none], axis=1), jnp.concatenate([none, second], axis=1)], axis=0
        ).astype(jnp.bfloat16)

        def piece_rows(q, columns_):
            parts = [
                slab[pl.ds(pl.multiple_of(b * 256 + (2 * q + i) * 16, 16), 16), columns_]
                for i in (0, 1)
                for b in range(8)
            ]
            return jnp.dot(picker, jnp.concatenate(parts, axis=0), preferred_element_type=jnp.float32)

        def columns(q, carry):
            stage[buffer, :, pl.ds(pl.multiple_of(q * SUB, SUB), SUB)] = piece_rows(
                q, data_of(pair)
            ).astype(jnp.bfloat16)
            return carry

        lax.fori_loop(0, QS, columns, 0)
        stored(pair).start()
        return picker

    def place_scales(pickers):
        for pair in range(PAIRS):
            parts = [
                slab[pl.ds(b * 256 + i * 16, 16), pl.ds(SCALES, 128)] for i in (0, 1) for b in range(8)
            ]
            scales[pl.ds(pair * 256, 256), :] = jnp.dot(
                pickers[pair], jnp.concatenate(parts, axis=0), preferred_element_type=jnp.float32
            )

    def stored(pair):
        return pltpu.make_async_copy(
            stage.at[pair % 2], placed.at[pl.ds(pair * 256, 256)], l_sem.at[2 + pair % 2]
        )

    first_sends()
    load_rows.wait()

    largest = jnp.zeros((HEADS, 1), jnp.float32)
    for q in range(QS):
        part = jnp.abs(rows[:, pl.ds(q * SUB, SUB)].astype(jnp.float32))
        largest = jnp.maximum(largest, jnp.max(part, axis=1, keepdims=True))
    row_scale = (largest + epsilon).astype(jnp.bfloat16)
    scale = row_scale.astype(jnp.float32)
    for q in range(QS):
        stacked[pl.ds(q * HEADS, HEADS), :] = (
            rows[:, pl.ds(q * SUB, SUB)].astype(jnp.float32) / scale
        ).astype(jnp.bfloat16)
    wide_scale = jnp.broadcast_to(scale, (HEADS, 128)).astype(jnp.bfloat16)

    def head_column(pair):
        row = lax.broadcasted_iota(jnp.int32, (256, 128), 0)
        lane = lax.broadcasted_iota(jnp.int32, (256, 128), 1)
        u, i = row // 16, row % 2
        if pair < 4:
            chosen = jnp.where(lane == u * 8 + 2 * pair + i, query_row[0:1, :], 0)
            return jnp.sum(chosen.astype(jnp.float32), axis=1, keepdims=True).astype(jnp.int32)
        row = lax.broadcasted_iota(jnp.int32, (256, 16), 0)
        lane = lax.broadcasted_iota(jnp.int32, (256, 16), 1)
        chosen = jnp.where(lane == row // 16, kv_row[0:1, :] + QH + KVH * (row % 2), 0)
        return jnp.sum(chosen.astype(jnp.float32), axis=1, keepdims=True).astype(jnp.int32)

    heads = [head_column(pair) for pair in range(PAIRS)]
    def prepare(pair):
        piece_of = (lax.broadcasted_iota(jnp.int32, (256, 1), 0) // 2) % QS
        want = heads[pair] + piece_of * HEADS
        lanes = lax.broadcasted_iota(jnp.int32, (256, QS * HEADS), 1)
        pick = jnp.where(lanes == want, 1.0, 0.0).astype(jnp.bfloat16)
        sending[:, data_of(pair)] = jnp.dot(
            pick, stacked[...], preferred_element_type=jnp.float32
        ).astype(jnp.bfloat16)

    for pair in range(PAIRS - 1):
        prepare(pair)
        scatter(pair)
        if pair == 1:
            token_step(0)
    tile = jnp.zeros((256, 128), jnp.float32)
    lane = lax.broadcasted_iota(jnp.int32, (256, HEADS), 1)
    lane128 = lax.broadcasted_iota(jnp.int32, (256, 128), 1)
    for pair in range(PAIRS):
        pick = jnp.where(lane == heads[pair], 1.0, 0.0).astype(jnp.bfloat16)
        got = jnp.dot(pick, wide_scale, preferred_element_type=jnp.float32)
        tile = jnp.where(lane128 == pair, got, tile)
    sending[:, pl.ds(SCALES, 128)] = tile.astype(jnp.bfloat16)

    prepare(PAIRS - 1)
    scatter(PAIRS - 1)

    turned[...] = jnp.zeros_like(turned)
    for i in range(GROUP):
        if i < 8:
            head = query_s[tp * 8 + i]
        else:
            head = kv_s[tp] + QH + KVH * (i - 8)
        slot = slots[pl.ds(head, 1), :]
        source = ((slot.astype(jnp.float32) + 0.5) * (1.0 / HEADS)).astype(jnp.int32)
        at = ((source // 16) % 2 * 4 + source // 32) * 16 + source % 16
        turned[i : i + 1, :] = at
    turned[...] = jnp.transpose(turned[...].astype(jnp.float32)).astype(jnp.int32)

    def angles():
        lines = jnp.concatenate(
            [position_rows[...].astype(jnp.float32), jnp.zeros((HD - 8, HD), jnp.float32)], axis=0
        )
        lines = jnp.transpose(lines)
        sign = jnp.where(lax.broadcasted_iota(jnp.int32, (HD, HD), 1) < HD // 2, -1.0, 1.0)
        for k in range(8):
            angle = lines[:, k : k + 1] * frequency[0:1, :]
            cosines[pl.ds(k * HD, HD), :] = jnp.cos(angle)
            sines[pl.ds(k * HD, HD), :] = jnp.sin(angle) * sign

    pickers = []
    gathered(0)
    token_step(1)
    gathered(1)
    token_step(2)
    relayed(0)
    gathered(2)
    token_step(3)
    angles()
    opposite(0)
    relayed(1)
    gathered(3)
    token_step(4)
    opposite(1)
    relayed(2)
    gathered(4)
    crossed(0)
    pickers.append(place(0))
    token_step(5)
    opposite(2)
    relayed(3)
    crossed(1)
    pickers.append(place(1))
    token_step(6)
    token_step(8)
    opposite(3)
    relayed(4)
    crossed(2)
    pickers.append(place(2))
    token_step(7)
    token_step(9)
    crossed(3)
    pickers.append(place(3))
    opposite(4)
    crossed(4)
    pickers.append(place(4))
    place_scales(pickers)
    token_step(10)
    token_step(11)

    own_copy.wait()
    stored(3).wait()
    stored(4).wait()
    for copy in started:
        copy.wait_send()
    for pair in range(PAIRS):
        fifteen = sending.at[pl.ds(0, 240), columns_of(pair)]
        pltpu.make_async_copy(fifteen, fifteen, a_send.at[pair]).wait()


def project(tokens, weight, scales, cosines, sines, refit, out, held, t_sem, r_sem):
    pair = pl.program_id(0)

    def load(k):
        return pltpu.make_async_copy(
            tokens.at[pl.ds(k * 256, 256)], held.at[pl.ds(k * 256, 256)], t_sem.at[k]
        )

    @pl.when(pair == 0)
    def _():
        for k in range(4):
            load(k).start()

    keep = pltpu.make_async_copy(weight, refit.at[pl.ds(pl.multiple_of(pair * 256, 256), 256)], r_sem)
    keep.start()

    lane = lax.broadcasted_iota(jnp.int32, (8, 128), 1)
    chosen = jnp.where(lane == pair, 1.0, 0.0).astype(jnp.bfloat16)
    column_scale = lax.dot_general(
        chosen,
        scales[...].astype(jnp.bfloat16),
        (((1,), (1,)), ((), ())),
        preferred_element_type=jnp.float32,
    )[0:1, :]

    @pl.when(pair == 0)
    def _():
        for k in range(4):
            load(k).wait()

    product = lax.dot_general(
        held[...], weight[...], (((1,), (1,)), ((), ())), preferred_element_type=jnp.float32
    )
    product = product * column_scale
    for i in (0, 1):
        part = product[:, i * HD : (i + 1) * HD]
        turn = part * cosines[...] + pltpu.roll(part, HD // 2, 1) * sines[...]
        if i == 1:
            turn = jnp.where(pair == PAIRS - 1, part, turn)
        out[:, pl.ds(i * HD, HD)] = turn.astype(jnp.bfloat16)
    keep.wait()


def per_device(learner_rows, learner_slot, query_order, kv_order, tokens, positions):
    any_space = pl.BlockSpec(memory_space=pl.ANY)
    vmem = pl.BlockSpec(memory_space=pltpu.VMEM)
    smem = pl.BlockSpec(memory_space=pltpu.SMEM)
    dma = pltpu.SemaphoreType.DMA
    frequency = jnp.exp(jnp.arange(HD // 2, dtype=jnp.float32) * (-2.0 * math.log(rope_base) / HD))
    all_tokens, placed, scales, cosines, sines = pl.pallas_call(
        exchange,
        out_shape=(
            jax.ShapeDtypeStruct((16, ROWS, DW), jnp.bfloat16),
            jax.ShapeDtypeStruct((GROUP * HD, DW), jnp.bfloat16),
            jax.ShapeDtypeStruct((GROUP * HD, 128), jnp.float32),
            jax.ShapeDtypeStruct((SPAN, HD), jnp.float32),
            jax.ShapeDtypeStruct((SPAN, HD), jnp.float32),
        ),
        in_specs=[any_space, any_space, vmem, vmem, vmem, smem, smem, vmem, vmem],
        out_specs=(any_space, any_space, vmem, vmem, vmem),
        scratch_shapes=[
            pltpu.VMEM((HEADS, DW), jnp.bfloat16),
            pltpu.VMEM((QS * HEADS, SUB), jnp.bfloat16),
            pltpu.VMEM((256, WIDE), jnp.bfloat16),
            pltpu.VMEM((256, WIDE), jnp.bfloat16),
            pltpu.VMEM((SLOTS, WIDE), jnp.bfloat16),
            pltpu.VMEM((2, 256, DW), jnp.bfloat16),
            pltpu.VMEM((HD, HD), jnp.int32),
            dma((40,)),
            dma((40,)),
            dma((40,)),
            dma((20,)),
            dma((PAIRS,)),
            dma((PAIRS,)),
            dma((PAIRS,)),
            dma((4,)),
            dma((PAIRS,)),
        ],
        compiler_params=pltpu.CompilerParams(
            collective_id=0, has_side_effects=True, vmem_limit_bytes=56 * 2**20
        ),
    )(
        tokens,
        learner_rows,
        learner_slot.reshape(HEADS, HD),
        query_order.reshape(1, QH),
        kv_order.reshape(1, 16),
        query_order,
        kv_order,
        positions.reshape(8, HD),
        jnp.concatenate([frequency, frequency]).reshape(1, HD),
    )

    return pl.pallas_call(
        project,
        grid=(PAIRS,),
        out_shape=(
            jax.ShapeDtypeStruct((GROUP * HD, DW), jnp.bfloat16),
            jax.ShapeDtypeStruct((SPAN, GROUP * HD), jnp.bfloat16),
        ),
        in_specs=[
            any_space,
            pl.BlockSpec((256, DW), lambda p: (p, 0)),
            pl.BlockSpec((256, 128), lambda p: (p, 0)),
            pl.BlockSpec((SPAN, HD), lambda p: (0, 0)),
            pl.BlockSpec((SPAN, HD), lambda p: (0, 0)),
        ],
        out_specs=(any_space, pl.BlockSpec((SPAN, 256), lambda p: (0, p))),
        scratch_shapes=[pltpu.VMEM((SPAN, DW), jnp.bfloat16), dma((4,)), dma],
        compiler_params=pltpu.CompilerParams(vmem_limit_bytes=56 * 2**20),
    )(all_tokens.reshape(SPAN, DW), placed, scales, cosines, sines)


def solution(mesh):
    in_specs = (P(("rep", "tp"), None), P(), P(), P(), P(("rep", "tp"), None), P("rep"))
    out_specs = (P("tp", None), P("rep", "tp"))
    return jax.shard_map(
        per_device, mesh=mesh, in_specs=in_specs, out_specs=out_specs, check_vma=False
    )
```

```python
import functools
import math

import jax
import jax.numpy as jnp
from jax import lax
from jax.experimental import pallas as pl
from jax.experimental.pallas import tpu as pltpu
from jax.sharding import PartitionSpec as P

HD = 128
QH = 128
KVH = 8
HEADS = 144
GROUP = 10
DW = 8192
SPAN = 1024
ROWS = 64
PAIRS = 5
SUB = 1024
QS = DW // SUB
HALF = DW // 2
WIDE = PAIRS * SUB + 128
SCALES = 2 * SUB
SLOTS = 2048

epsilon = 1e-06
rope_base = 500000.0
MESH = pl.DeviceIdType.MESH


def columns_of(pair):
    return pl.ds(pair * SUB + (128 if pair > 1 else 0), SUB + 128 if pair == 1 else SUB)


def data_of(pair):
    return pl.ds(pair * SUB + (128 if pair > 1 else 0), SUB)


def place_at(x, z, dx, dz):
    return lax.rem(x + dx + 4, 4) * 4 + lax.rem(z + dz + 4, 4)


EARLY = ((0, 0), (1, 0), (-1, 0), (0, 1), (0, -1), (-1, -1), (1, 1), (1, -1), (-1, 1))
LATE = ((2, 0), (0, 2), (2, -1), (2, 1), (-1, 2), (1, 2), (2, 2))
E_ROWS = len(EARLY) * ROWS
L_ROWS = len(LATE) * ROWS


def rotated(product, scale, cosines, sines, is_value):
    parts = []
    for i in (0, 1):
        part = product[:, i * HD : (i + 1) * HD] * scale[:, i * HD : (i + 1) * HD]
        turn = part * cosines + pltpu.roll(part, HD // 2, 1) * sines
        parts.append(turn if i == 0 else jnp.where(is_value, part, turn))
    return parts


def exchange(
    tokens,
    learner,
    slots,
    query_row,
    kv_row,
    query_s,
    kv_s,
    position_rows,
    frequency,
    all_tokens,
    placed,
    scale_rows,
    early,
    cosines_late,
    sines_late,
    rows,
    stacked,
    sending,
    arrived,
    slab,
    stage,
    turned,
    pickers,
    cosines,
    sines,
    cosines_early,
    sines_early,
    held,
    result,
    t_send,
    t_recv,
    w_send,
    w_recv,
    a_send,
    a_recv,
    c_recv,
    l_sem,
    s_sem,
    e_sem,
    o_sem,
):
    rep = lax.axis_index("rep")
    tp = lax.axis_index("tp")
    y, core = rep // 2, rep % 2
    x, z = tp // 4, tp % 4

    def place_of(dx, dz):
        return place_at(x, z, dx, dz)

    def rep_of(dy):
        return lax.rem(y + dy + 4, 4) * 2 + core

    twin = y * 2 + 1 - core

    load_rows = pltpu.make_async_copy(learner, rows, l_sem.at[0])
    load_rows.start()
    own_copy = pltpu.make_async_copy(tokens, all_tokens.at[tp], l_sem.at[1])
    own_copy.start()

    barrier = pltpu.get_barrier_semaphore()
    offsets = [(dx, dz) for dx in (1, 3, 0, 2) for dz in (1, 3, 0, 2) if (dx, dz) != (0, 0)]
    for dx, dz in offsets:
        pl.semaphore_signal(barrier, inc=1, device_id=(rep, place_of(dx, dz)), device_id_type=MESH)
    for other in (rep_of(1), rep_of(3), twin):
        pl.semaphore_signal(barrier, inc=1, device_id=(other, tp), device_id_type=MESH)
    pl.semaphore_wait(barrier, len(offsets) + 3)

    def along(half, phase, step):
        return place_of(step, 0) if (half == 0) == (phase == 0) else place_of(0, step)

    def block_at(half, first, second):
        return place_of(first, second) if half == 0 else place_of(second, first)

    def piece(ref, half, low, count):
        return ref.at[pl.ds(low, count), pl.ds(half * HALF, HALF)]

    started = []

    def token_copy(half, number, block, low, count, phase, step, own=False):
        k = half * 22 + number
        source = piece(tokens, half, low, count) if own else piece(all_tokens.at[block], half, low, count)
        copy = pltpu.make_async_remote_copy(
            src_ref=source,
            dst_ref=piece(all_tokens.at[block], half, low, count),
            send_sem=t_send.at[k],
            recv_sem=t_recv.at[k],
            device_id=(rep, along(half, phase, step)),
            device_id_type=MESH,
        )
        copy.start()
        started.append(copy)

    def token_wait(half, number, block, low, count):
        k = half * 22 + number
        here = piece(all_tokens.at[block], half, low, count)
        pltpu.make_async_copy(here, here, t_recv.at[k]).wait()

    def first_sends(part):
        low = part * ROWS // 2
        for half in (0, 1):
            token_copy(half, 20 * part, tp, low, ROWS // 2, 0, 1, own=True)
            token_copy(half, 20 * part + 1, tp, low, ROWS // 2, 0, -1, own=True)

    order = (0, -1, 1, 2)

    def second_sends(half, k):
        block = block_at(half, order[k], 0)
        token_copy(half, 4 + 4 * k, block, 0, ROWS, 1, 1, own=k == 0)
        token_copy(half, 5 + 4 * k, block, 0, ROWS, 1, -1, own=k == 0)

    def token_step(number):
        for half in (0, 1):
            if number == 0:
                second_sends(half, 0)
            elif number == 1:
                block = block_at(half, -1, 0)
                token_wait(half, 0, block, 0, ROWS // 2)
                token_wait(half, 20, block, ROWS // 2, ROWS // 2)
                token_copy(half, 2, block, 0, ROWS // 2, 0, 1)
                second_sends(half, 1)
            elif number == 2:
                block = block_at(half, 1, 0)
                token_wait(half, 1, block, 0, ROWS // 2)
                token_wait(half, 21, block, ROWS // 2, ROWS // 2)
                token_copy(half, 3, block, ROWS // 2, ROWS // 2, 0, -1)
                second_sends(half, 2)
            elif number == 3:
                block = block_at(half, 2, 0)
                token_wait(half, 2, block, 0, ROWS // 2)
                token_wait(half, 3, block, ROWS // 2, ROWS // 2)
                second_sends(half, 3)
            elif number < 8:
                k = number - 4
                block = block_at(half, order[k], -1)
                token_wait(half, 4 + 4 * k, block, 0, ROWS)
                token_copy(half, 6 + 4 * k, block, 0, ROWS // 2, 1, 1)
                block = block_at(half, order[k], 1)
                token_wait(half, 5 + 4 * k, block, 0, ROWS)
                token_copy(half, 7 + 4 * k, block, ROWS // 2, ROWS // 2, 1, -1)
            else:
                k = number - 8
                block = block_at(half, order[k], 2)
                token_wait(half, 6 + 4 * k, block, 0, ROWS // 2)
                token_wait(half, 7 + 4 * k, block, ROWS // 2, ROWS // 2)

    def block_rows(core_, y_, low=0, count=256):
        return pl.ds(pl.multiple_of((core_ * 4 + y_) * 256, 256) + low, count)

    mine = block_rows(core, y)

    def weight_copy(pair, number, rows_, recv, device):
        k = pair * 8 + number
        here = slab.at[rows_, columns_of(pair)]
        copy = pltpu.make_async_remote_copy(
            src_ref=here, dst_ref=here, send_sem=w_send.at[k], recv_sem=recv, device_id=device, device_id_type=MESH
        )
        copy.start()
        started.append(copy)

    def weight_wait(pair, rows_, sem):
        here = slab.at[rows_, columns_of(pair)]
        pltpu.make_async_copy(here, here, sem).wait()

    def scatter(pair):
        for dx, dz in offsets:
            to = place_of(dx, dz)
            pltpu.make_async_remote_copy(
                src_ref=sending.at[pl.ds(pl.multiple_of(to * 16, 16), 16), columns_of(pair)],
                dst_ref=arrived.at[pl.ds(pl.multiple_of(tp * 16, 16), 16), columns_of(pair)],
                send_sem=a_send.at[pair],
                recv_sem=a_recv.at[pair],
                device_id=(rep, to),
                device_id_type=MESH,
            ).start()
        pltpu.make_async_copy(
            sending.at[pl.ds(pl.multiple_of(tp * 16, 16), 16), columns_of(pair)],
            arrived.at[pl.ds(pl.multiple_of(tp * 16, 16), 16), columns_of(pair)],
            s_sem.at[pair],
        ).start()

    ym, yp, y2 = lax.rem(y + 3, 4), lax.rem(y + 1, 4), lax.rem(y + 2, 4)
    up, down, across = (rep_of(1), tp), (rep_of(-1), tp), (twin, tp)

    def gathered(pair):
        fifteen = arrived.at[pl.ds(0, 240), columns_of(pair)]
        pltpu.make_async_copy(fifteen, fifteen, a_recv.at[pair]).wait()
        one = arrived.at[pl.ds(0, 16), columns_of(pair)]
        pltpu.make_async_copy(one, one, s_sem.at[pair]).wait()
        row = lax.broadcasted_iota(jnp.int32, (256, 256), 0)
        lane = lax.broadcasted_iota(jnp.int32, (256, 256), 1)
        swap = jnp.where(lane == (row % 16) * 16 + row // 16, 1.0, 0.0).astype(jnp.bfloat16)
        slab[mine, columns_of(pair)] = jnp.dot(
            swap, arrived[:, columns_of(pair)], preferred_element_type=jnp.float32
        ).astype(jnp.bfloat16)
        weight_copy(pair, 0, mine, w_recv.at[pair * 4], up)
        weight_copy(pair, 1, mine, w_recv.at[pair * 4 + 1], down)
        weight_copy(pair, 4, mine, c_recv.at[pair], across)

    def relayed(pair):
        weight_wait(pair, block_rows(core, ym), w_recv.at[pair * 4])
        weight_copy(pair, 2, block_rows(core, ym, 0, 128), w_recv.at[pair * 4 + 2], up)
        weight_copy(pair, 5, block_rows(core, ym), c_recv.at[pair], across)
        weight_wait(pair, block_rows(core, yp), w_recv.at[pair * 4 + 1])
        weight_copy(pair, 3, block_rows(core, yp, 128, 128), w_recv.at[pair * 4 + 3], down)
        weight_copy(pair, 6, block_rows(core, yp), c_recv.at[pair], across)

    def opposite(pair):
        weight_wait(pair, block_rows(core, y2, 0, 128), w_recv.at[pair * 4 + 2])
        weight_wait(pair, block_rows(core, y2, 128, 128), w_recv.at[pair * 4 + 3])
        weight_copy(pair, 7, block_rows(core, y2), c_recv.at[pair], across)

    def crossed(pair):
        weight_wait(pair, pl.ds(pl.multiple_of((1 - core) * 1024, 1024), 1024), c_recv.at[pair])

    def place(pair):
        buffer = pair % 2
        if pair >= 2:
            stored(pair - 2).wait()

        def piece_rows(q, columns_):
            parts = [
                slab[pl.ds(pl.multiple_of(b * 256 + (2 * q + i) * 16, 16), 16), columns_]
                for i in (0, 1)
                for b in range(8)
            ]
            return jnp.dot(pickers[pair], jnp.concatenate(parts, axis=0), preferred_element_type=jnp.float32)

        def columns(q, carry):
            stage[buffer, :, pl.ds(pl.multiple_of(q * SUB, SUB), SUB)] = piece_rows(
                q, data_of(pair)
            ).astype(jnp.bfloat16)
            return carry

        lax.fori_loop(0, QS, columns, 0)
        stored(pair).start()

    def make_pickers():
        lane = lax.broadcasted_iota(jnp.int32, (HD, HD), 1)
        none = jnp.zeros((HD, HD), jnp.float32)
        for pair in range(PAIRS):
            first = jnp.where(lane == turned[:, 2 * pair : 2 * pair + 1], 1.0, 0.0)
            second = jnp.where(lane == turned[:, 2 * pair + 1 : 2 * pair + 2], 1.0, 0.0)
            pickers[pair] = jnp.concatenate(
                [jnp.concatenate([first, none], axis=1), jnp.concatenate([none, second], axis=1)], axis=0
            ).astype(jnp.bfloat16)

    def place_scales():
        lane = lax.broadcasted_iota(jnp.int32, (8, 128), 1)
        parts = [slab[pl.ds(b * 256 + i * 16, 16), pl.ds(SCALES, 128)] for i in (0, 1) for b in range(8)]
        tiles = jnp.concatenate(parts, axis=0)
        for pair in range(PAIRS):
            column = jnp.dot(pickers[pair], tiles, preferred_element_type=jnp.float32)
            chosen = jnp.where(lane == pair, 1.0, 0.0).astype(jnp.bfloat16)
            scale_rows[pl.ds(pair * 8, 8), :] = lax.dot_general(
                chosen,
                column.astype(jnp.bfloat16),
                (((1,), (1,)), ((), ())),
                preferred_element_type=jnp.float32,
            )

    def early_load(k):
        block = place_of(*EARLY[k])
        return pltpu.make_async_copy(all_tokens.at[block], held.at[pl.ds(k * ROWS, ROWS)], e_sem.at[k])

    def load_early(low, high):
        if low == 0:
            own_copy.wait()
        for k in range(low, high):
            early_load(k).start()

    def early_out(pair):
        return pltpu.make_async_copy(
            result.at[pair % 2], early.at[:, pl.ds(pair * 256, 256)], o_sem.at[pair % 2]
        )

    def multiply(pair):
        if pair == 0:
            for k in range(len(EARLY)):
                early_load(k).wait()
        if pair >= 2:
            early_out(pair - 2).wait()
        product = lax.dot_general(
            held[...], stage[pair % 2], (((1,), (1,)), ((), ())), preferred_element_type=jnp.float32
        )
        parts = rotated(
            product,
            scale_rows[pl.ds(pair * 8, 1), :],
            cosines_early[...],
            sines_early[...],
            pair == PAIRS - 1,
        )
        for i in (0, 1):
            result[pair % 2, :, pl.ds(i * HD, HD)] = parts[i].astype(jnp.bfloat16)
        early_out(pair).start()

    def stored(pair):
        return pltpu.make_async_copy(
            stage.at[pair % 2], placed.at[pl.ds(pair * 256, 256)], l_sem.at[2 + pair % 2]
        )

    first_sends(0)
    load_rows.wait()

    largest = jnp.zeros((HEADS, 1), jnp.float32)
    for q in range(QS):
        part = jnp.abs(rows[:, pl.ds(q * SUB, SUB)].astype(jnp.float32))
        largest = jnp.maximum(largest, jnp.max(part, axis=1, keepdims=True))
    row_scale = (largest + epsilon).astype(jnp.bfloat16)
    scale = row_scale.astype(jnp.float32)
    for q in range(QS):
        stacked[pl.ds(q * HEADS, HEADS), :] = (
            rows[:, pl.ds(q * SUB, SUB)].astype(jnp.float32) / scale
        ).astype(jnp.bfloat16)
    wide_scale = jnp.broadcast_to(scale, (HEADS, 128)).astype(jnp.bfloat16)

    def head_column(pair):
        row = lax.broadcasted_iota(jnp.int32, (256, 128), 0)
        lane = lax.broadcasted_iota(jnp.int32, (256, 128), 1)
        u, i = row // 16, row % 2
        if pair < 4:
            chosen = jnp.where(lane == u * 8 + 2 * pair + i, query_row[0:1, :], 0)
            return jnp.sum(chosen.astype(jnp.float32), axis=1, keepdims=True).astype(jnp.int32)
        row = lax.broadcasted_iota(jnp.int32, (256, 16), 0)
        lane = lax.broadcasted_iota(jnp.int32, (256, 16), 1)
        chosen = jnp.where(lane == row // 16, kv_row[0:1, :] + QH + KVH * (row % 2), 0)
        return jnp.sum(chosen.astype(jnp.float32), axis=1, keepdims=True).astype(jnp.int32)

    heads = [head_column(pair) for pair in range(PAIRS)]
    def prepare(pair):
        piece_of = (lax.broadcasted_iota(jnp.int32, (256, 1), 0) // 2) % QS
        want = heads[pair] + piece_of * HEADS
        lanes = lax.broadcasted_iota(jnp.int32, (256, QS * HEADS), 1)
        pick = jnp.where(lanes == want, 1.0, 0.0).astype(jnp.bfloat16)
        sending[:, data_of(pair)] = jnp.dot(
            pick, stacked[...], preferred_element_type=jnp.float32
        ).astype(jnp.bfloat16)

    prepare(0)
    scatter(0)
    first_sends(1)
    tile = jnp.zeros((256, 128), jnp.float32)
    lane = lax.broadcasted_iota(jnp.int32, (256, HEADS), 1)
    lane128 = lax.broadcasted_iota(jnp.int32, (256, 128), 1)
    for pair in range(PAIRS):
        pick = jnp.where(lane == heads[pair], 1.0, 0.0).astype(jnp.bfloat16)
        got = jnp.dot(pick, wide_scale, preferred_element_type=jnp.float32)
        tile = jnp.where(lane128 == pair, got, tile)
    sending[:, pl.ds(SCALES, 128)] = tile.astype(jnp.bfloat16)

    prepare(1)
    scatter(1)
    prepare(2)
    scatter(2)
    prepare(3)
    scatter(3)
    prepare(4)
    scatter(4)
    token_step(0)

    turned[...] = jnp.zeros_like(turned)
    for i in range(GROUP):
        if i < 8:
            head = query_s[tp * 8 + i]
        else:
            head = kv_s[tp] + QH + KVH * (i - 8)
        slot = slots[pl.ds(head, 1), :]
        source = ((slot.astype(jnp.float32) + 0.5) * (1.0 / HEADS)).astype(jnp.int32)
        at = ((source // 16) % 2 * 4 + source // 32) * 16 + source % 16
        turned[i : i + 1, :] = at
    turned[...] = jnp.transpose(turned[...].astype(jnp.float32)).astype(jnp.int32)

    def angles():
        lines = jnp.concatenate(
            [position_rows[...].astype(jnp.float32), jnp.zeros((HD - 8, HD), jnp.float32)], axis=0
        )
        lines = jnp.transpose(lines)
        sign = jnp.where(lax.broadcasted_iota(jnp.int32, (HD, HD), 1) < HD // 2, -1.0, 1.0)
        for k in range(8):
            angle = lines[:, k : k + 1] * frequency[0:1, :]
            cosines[pl.ds(k * HD, HD), :] = jnp.cos(angle)
            sines[pl.ds(k * HD, HD), :] = jnp.sin(angle) * sign
        for blocks, c_ref, s_ref in (
            (EARLY, cosines_early, sines_early),
            (LATE, cosines_late, sines_late),
        ):
            for k, offset in enumerate(blocks):
                there = pl.ds(pl.multiple_of(place_of(*offset) * ROWS, ROWS), ROWS)
                c_ref[pl.ds(k * ROWS, ROWS), :] = cosines[there, :]
                s_ref[pl.ds(k * ROWS, ROWS), :] = sines[there, :]

    make_pickers()
    token_step(1)
    token_step(2)
    gathered(0)
    gathered(1)
    gathered(2)
    relayed(0)
    gathered(3)
    angles()
    relayed(1)
    gathered(4)
    relayed(2)
    token_step(4)
    opposite(0)
    crossed(0)
    place(0)
    relayed(3)
    token_step(3)
    token_step(5)
    opposite(1)
    crossed(1)
    place(1)
    place_scales()
    token_step(6)
    load_early(0,9)
    relayed(4)
    multiply(0)
    multiply(1)
    token_step(8)
    opposite(2)
    crossed(2)
    place(2)
    token_step(7)
    multiply(2)
    opposite(3)
    crossed(3)
    place(3)
    multiply(3)
    opposite(4)
    crossed(4)
    place(4)
    multiply(4)
    token_step(9)
    token_step(10)
    token_step(11)

    stored(3).wait()
    stored(4).wait()
    early_out(3).wait()
    early_out(4).wait()
    for copy in started:
        copy.wait_send()
    for pair in range(PAIRS):
        fifteen = sending.at[pl.ds(0, 240), columns_of(pair)]
        pltpu.make_async_copy(fifteen, fifteen, a_send.at[pair]).wait()


def project(tokens, weight, scale_rows, early, cosines, sines, refit, out, held, t_sem, r_sem):
    pair = pl.program_id(0)
    tp = lax.axis_index("tp")
    x, z = tp // 4, tp % 4

    def load(k):
        return pltpu.make_async_copy(
            tokens.at[place_at(x, z, *LATE[k])], held.at[pl.ds(k * ROWS, ROWS)], t_sem.at[k]
        )

    @pl.when(pair == 0)
    def _():
        for k in range(len(LATE)):
            load(k).start()

    keep = pltpu.make_async_copy(weight, refit.at[pl.ds(pl.multiple_of(pair * 256, 256), 256)], r_sem)
    keep.start()

    def rows_at(offset):
        return pl.ds(pl.multiple_of(place_at(x, z, *offset) * ROWS, ROWS), ROWS)

    for k, offset in enumerate(EARLY):
        out[rows_at(offset), :] = early[pl.ds(k * ROWS, ROWS), :]

    @pl.when(pair == 0)
    def _():
        for k in range(len(LATE)):
            load(k).wait()

    product = lax.dot_general(
        held[...], weight[...], (((1,), (1,)), ((), ())), preferred_element_type=jnp.float32
    )
    parts = rotated(product, scale_rows[0:1, :], cosines[...], sines[...], pair == PAIRS - 1)
    for i in (0, 1):
        part = parts[i].astype(jnp.bfloat16)
        for k, offset in enumerate(LATE):
            out[rows_at(offset), pl.ds(i * HD, HD)] = part[k * ROWS : (k + 1) * ROWS]
    keep.wait()


def per_device(learner_rows, learner_slot, query_order, kv_order, tokens, positions):
    any_space = pl.BlockSpec(memory_space=pl.ANY)
    vmem = pl.BlockSpec(memory_space=pltpu.VMEM)
    smem = pl.BlockSpec(memory_space=pltpu.SMEM)
    dma = pltpu.SemaphoreType.DMA
    frequency = jnp.exp(jnp.arange(HD // 2, dtype=jnp.float32) * (-2.0 * math.log(rope_base) / HD))
    all_tokens, placed, scale_rows, early, cosines, sines = pl.pallas_call(
        exchange,
        out_shape=(
            jax.ShapeDtypeStruct((16, ROWS, DW), jnp.bfloat16),
            jax.ShapeDtypeStruct((GROUP * HD, DW), jnp.bfloat16),
            jax.ShapeDtypeStruct((PAIRS * 8, 256), jnp.float32),
            jax.ShapeDtypeStruct((E_ROWS, GROUP * HD), jnp.bfloat16),
            jax.ShapeDtypeStruct((L_ROWS, HD), jnp.float32),
            jax.ShapeDtypeStruct((L_ROWS, HD), jnp.float32),
        ),
        in_specs=[any_space, any_space, vmem, vmem, vmem, smem, smem, vmem, vmem],
        out_specs=(any_space, any_space, vmem, any_space, vmem, vmem),
        scratch_shapes=[
            pltpu.VMEM((HEADS, DW), jnp.bfloat16),
            pltpu.VMEM((QS * HEADS, SUB), jnp.bfloat16),
            pltpu.VMEM((256, WIDE), jnp.bfloat16),
            pltpu.VMEM((256, WIDE), jnp.bfloat16),
            pltpu.VMEM((SLOTS, WIDE), jnp.bfloat16),
            pltpu.VMEM((2, 256, DW), jnp.bfloat16),
            pltpu.VMEM((HD, HD), jnp.int32),
            pltpu.VMEM((PAIRS, 256, 256), jnp.bfloat16),
            pltpu.VMEM((SPAN, HD), jnp.float32),
            pltpu.VMEM((SPAN, HD), jnp.float32),
            pltpu.VMEM((E_ROWS, HD), jnp.float32),
            pltpu.VMEM((E_ROWS, HD), jnp.float32),
            pltpu.VMEM((E_ROWS, DW), jnp.bfloat16),
            pltpu.VMEM((2, E_ROWS, 256), jnp.bfloat16),
            dma((44,)),
            dma((44,)),
            dma((40,)),
            dma((20,)),
            dma((PAIRS,)),
            dma((PAIRS,)),
            dma((PAIRS,)),
            dma((4,)),
            dma((PAIRS,)),
            dma((len(EARLY),)),
            dma((2,)),
        ],
        compiler_params=pltpu.CompilerParams(
            collective_id=0, has_side_effects=True, vmem_limit_bytes=62 * 2**20
        ),
    )(
        tokens,
        learner_rows,
        learner_slot.reshape(HEADS, HD),
        query_order.reshape(1, QH),
        kv_order.reshape(1, 16),
        query_order,
        kv_order,
        positions.reshape(8, HD),
        jnp.concatenate([frequency, frequency]).reshape(1, HD),
    )

    return pl.pallas_call(
        project,
        grid=(PAIRS,),
        out_shape=(
            jax.ShapeDtypeStruct((GROUP * HD, DW), jnp.bfloat16),
            jax.ShapeDtypeStruct((SPAN, GROUP * HD), jnp.bfloat16),
        ),
        in_specs=[
            any_space,
            pl.BlockSpec((256, DW), lambda p: (p, 0)),
            pl.BlockSpec((8, 256), lambda p: (p, 0)),
            pl.BlockSpec((E_ROWS, 256), lambda p: (0, p)),
            pl.BlockSpec((L_ROWS, HD), lambda p: (0, 0)),
            pl.BlockSpec((L_ROWS, HD), lambda p: (0, 0)),
        ],
        out_specs=(any_space, pl.BlockSpec((SPAN, 256), lambda p: (0, p))),
        scratch_shapes=[pltpu.VMEM((L_ROWS, DW), jnp.bfloat16), dma((len(LATE),)), dma],
        compiler_params=pltpu.CompilerParams(vmem_limit_bytes=62 * 2**20),
    )(all_tokens, placed, scale_rows, early, cosines, sines)


def solution(mesh):
    in_specs = (P(("rep", "tp"), None), P(), P(), P(), P(("rep", "tp"), None), P("rep"))
    out_specs = (P("tp", None), P("rep", "tp"))
    return jax.shard_map(
        per_device, mesh=mesh, in_specs=in_specs, out_specs=out_specs, check_vma=False
    )
```

```python
import functools
import math

import jax
import jax.numpy as jnp
import numpy as np
from jax import lax
from jax.experimental import pallas as pl
from jax.experimental.pallas import tpu as pltpu
from jax.sharding import PartitionSpec as P

HD = 128
QH = 128
KVH = 8
HEADS = 144
GROUP = 10
DW = 8192
SPAN = 1024
ROWS = 64
PAIRS = 5
SUB = 1024
QS = DW // SUB
HALF = DW // 2
WIDE = PAIRS * SUB + 128
SCALES = 2 * SUB
SLOTS = 2048

epsilon = 1e-06
rope_base = 500000.0
MESH = pl.DeviceIdType.MESH


def columns_of(pair):
    return pl.ds(pair * SUB + (128 if pair > 1 else 0), SUB + 128 if pair == 1 else SUB)


def data_of(pair):
    return pl.ds(pair * SUB + (128 if pair > 1 else 0), SUB)


def place_at(x, z, dx, dz):
    return lax.rem(x + dx + 4, 4) * 4 + lax.rem(z + dz + 4, 4)


EARLY = ((0, 0), (1, 0), (-1, 0), (0, 1), (0, -1), (-1, -1), (1, 1), (1, -1), (-1, 1))
LATE = ((2, 0), (0, 2), (2, -1), (2, 1), (-1, 2), (1, 2), (2, 2))
E_ROWS = len(EARLY) * ROWS
L_ROWS = len(LATE) * ROWS


def rotated(product, scale, cosines, sines, is_value):
    parts = []
    for i in (0, 1):
        part = product[:, i * HD : (i + 1) * HD] * scale[:, i * HD : (i + 1) * HD]
        turn = part * cosines + pltpu.roll(part, HD // 2, 1) * sines
        parts.append(turn if i == 0 else jnp.where(is_value, part, turn))
    return parts


def exchange(
    tokens,
    learner,
    slots,
    query_row,
    kv_row,
    query_s,
    kv_s,
    position_rows,
    frequency,
    all_tokens,
    placed,
    scale_rows,
    early,
    cosines_late,
    sines_late,
    rows,
    stacked,
    sending,
    arrived,
    slab,
    stage,
    turned,
    pickers,
    cosines,
    sines,
    cosines_early,
    sines_early,
    held,
    result,
    t_send,
    t_recv,
    w_send,
    w_recv,
    a_send,
    a_recv,
    c_recv,
    l_sem,
    s_sem,
    e_sem,
    o_sem,
):
    rep = lax.axis_index("rep")
    tp = lax.axis_index("tp")
    y, core = rep // 2, rep % 2
    x, z = tp // 4, tp % 4

    def place_of(dx, dz):
        return place_at(x, z, dx, dz)

    def rep_of(dy):
        return lax.rem(y + dy + 4, 4) * 2 + core

    twin = y * 2 + 1 - core

    load_rows = pltpu.make_async_copy(learner, rows, l_sem.at[0])
    load_rows.start()

    barrier = pltpu.get_barrier_semaphore()
    offsets = [(dx, dz) for dx in (1, 3, 0, 2) for dz in (1, 3, 0, 2) if (dx, dz) != (0, 0)]
    for dx, dz in offsets:
        pl.semaphore_signal(barrier, inc=1, device_id=(rep, place_of(dx, dz)), device_id_type=MESH)
    for other in (rep_of(1), rep_of(3), twin):
        pl.semaphore_signal(barrier, inc=1, device_id=(other, tp), device_id_type=MESH)
    pl.semaphore_wait(barrier, len(offsets) + 3)

    def along(half, phase, step):
        return place_of(step, 0) if (half == 0) == (phase == 0) else place_of(0, step)

    def block_at(half, first, second):
        return place_of(first, second) if half == 0 else place_of(second, first)

    def piece(ref, half, low, count):
        return ref.at[pl.ds(low, count), pl.ds(half * HALF, HALF)]

    started = []

    def token_copy(half, number, block, low, count, phase, step, own=False):
        k = half * 22 + number
        source = piece(tokens, half, low, count) if own else piece(all_tokens.at[block], half, low, count)
        copy = pltpu.make_async_remote_copy(
            src_ref=source,
            dst_ref=piece(all_tokens.at[block], half, low, count),
            send_sem=t_send.at[k],
            recv_sem=t_recv.at[k],
            device_id=(rep, along(half, phase, step)),
            device_id_type=MESH,
        )
        copy.start()
        started.append(copy)

    def token_wait(half, number, block, low, count):
        k = half * 22 + number
        here = piece(all_tokens.at[block], half, low, count)
        pltpu.make_async_copy(here, here, t_recv.at[k]).wait()

    def first_sends(part):
        low = part * ROWS // 2
        for half in (0, 1):
            token_copy(half, 20 * part, tp, low, ROWS // 2, 0, 1, own=True)
            token_copy(half, 20 * part + 1, tp, low, ROWS // 2, 0, -1, own=True)

    order = (0, -1, 1, 2)

    def second_sends(half, k):
        block = block_at(half, order[k], 0)
        token_copy(half, 4 + 4 * k, block, 0, ROWS, 1, 1, own=k == 0)
        token_copy(half, 5 + 4 * k, block, 0, ROWS, 1, -1, own=k == 0)

    def token_step(number):
        for half in (0, 1):
            if number == 0:
                second_sends(half, 0)
            elif number == 1:
                block = block_at(half, -1, 0)
                token_wait(half, 0, block, 0, ROWS // 2)
                token_wait(half, 20, block, ROWS // 2, ROWS // 2)
                token_copy(half, 2, block, 0, ROWS // 2, 0, 1)
                second_sends(half, 1)
            elif number == 2:
                block = block_at(half, 1, 0)
                token_wait(half, 1, block, 0, ROWS // 2)
                token_wait(half, 21, block, ROWS // 2, ROWS // 2)
                token_copy(half, 3, block, ROWS // 2, ROWS // 2, 0, -1)
                second_sends(half, 2)
            elif number == 3:
                block = block_at(half, 2, 0)
                token_wait(half, 2, block, 0, ROWS // 2)
                token_wait(half, 3, block, ROWS // 2, ROWS // 2)
                second_sends(half, 3)
            elif number < 8:
                k = number - 4
                block = block_at(half, order[k], -1)
                token_wait(half, 4 + 4 * k, block, 0, ROWS)
                token_copy(half, 6 + 4 * k, block, 0, ROWS // 2, 1, 1)
                block = block_at(half, order[k], 1)
                token_wait(half, 5 + 4 * k, block, 0, ROWS)
                token_copy(half, 7 + 4 * k, block, ROWS // 2, ROWS // 2, 1, -1)
            else:
                k = number - 8
                block = block_at(half, order[k], 2)
                token_wait(half, 6 + 4 * k, block, 0, ROWS // 2)
                token_wait(half, 7 + 4 * k, block, ROWS // 2, ROWS // 2)

    def block_rows(core_, y_, low=0, count=256):
        return pl.ds(pl.multiple_of((core_ * 4 + y_) * 256, 256) + low, count)

    mine = block_rows(core, y)

    def weight_copy(pair, number, rows_, recv, device):
        k = pair * 8 + number
        here = slab.at[rows_, columns_of(pair)]
        copy = pltpu.make_async_remote_copy(
            src_ref=here, dst_ref=here, send_sem=w_send.at[k], recv_sem=recv, device_id=device, device_id_type=MESH
        )
        copy.start()
        started.append(copy)

    def weight_wait(pair, rows_, sem):
        here = slab.at[rows_, columns_of(pair)]
        pltpu.make_async_copy(here, here, sem).wait()

    def scatter(pair):
        for dx, dz in offsets:
            to = place_of(dx, dz)
            pltpu.make_async_remote_copy(
                src_ref=sending.at[pl.ds(pl.multiple_of(to * 16, 16), 16), columns_of(pair)],
                dst_ref=arrived.at[pl.ds(pl.multiple_of(tp * 16, 16), 16), columns_of(pair)],
                send_sem=a_send.at[pair],
                recv_sem=a_recv.at[pair],
                device_id=(rep, to),
                device_id_type=MESH,
            ).start()
        pltpu.make_async_copy(
            sending.at[pl.ds(pl.multiple_of(tp * 16, 16), 16), columns_of(pair)],
            arrived.at[pl.ds(pl.multiple_of(tp * 16, 16), 16), columns_of(pair)],
            s_sem.at[pair],
        ).start()

    ym, yp, y2 = lax.rem(y + 3, 4), lax.rem(y + 1, 4), lax.rem(y + 2, 4)
    up, down, across = (rep_of(1), tp), (rep_of(-1), tp), (twin, tp)

    def gathered(pair):
        fifteen = arrived.at[pl.ds(0, 240), columns_of(pair)]
        pltpu.make_async_copy(fifteen, fifteen, a_recv.at[pair]).wait()
        one = arrived.at[pl.ds(0, 16), columns_of(pair)]
        pltpu.make_async_copy(one, one, s_sem.at[pair]).wait()
        row = lax.broadcasted_iota(jnp.int32, (256, 256), 0)
        lane = lax.broadcasted_iota(jnp.int32, (256, 256), 1)
        swap = jnp.where(lane == (row % 16) * 16 + row // 16, 1.0, 0.0).astype(jnp.bfloat16)
        slab[mine, columns_of(pair)] = jnp.dot(
            swap, arrived[:, columns_of(pair)], preferred_element_type=jnp.float32
        ).astype(jnp.bfloat16)
        weight_copy(pair, 0, mine, w_recv.at[pair * 4], up)
        weight_copy(pair, 1, mine, w_recv.at[pair * 4 + 1], down)
        weight_copy(pair, 4, mine, c_recv.at[pair], across)

    def relayed(pair):
        weight_wait(pair, block_rows(core, ym), w_recv.at[pair * 4])
        weight_copy(pair, 2, block_rows(core, ym, 0, 128), w_recv.at[pair * 4 + 2], up)
        weight_copy(pair, 5, block_rows(core, ym), c_recv.at[pair], across)
        weight_wait(pair, block_rows(core, yp), w_recv.at[pair * 4 + 1])
        weight_copy(pair, 3, block_rows(core, yp, 128, 128), w_recv.at[pair * 4 + 3], down)
        weight_copy(pair, 6, block_rows(core, yp), c_recv.at[pair], across)

    def opposite(pair):
        weight_wait(pair, block_rows(core, y2, 0, 128), w_recv.at[pair * 4 + 2])
        weight_wait(pair, block_rows(core, y2, 128, 128), w_recv.at[pair * 4 + 3])
        weight_copy(pair, 7, block_rows(core, y2), c_recv.at[pair], across)

    def crossed(pair):
        weight_wait(pair, pl.ds(pl.multiple_of((1 - core) * 1024, 1024), 1024), c_recv.at[pair])

    def place(pair):
        buffer = pair % 2
        if pair >= 2:
            stored(pair - 2).wait()

        def piece_rows(q, columns_):
            parts = [
                slab[pl.ds(pl.multiple_of(b * 256 + (2 * q + i) * 16, 16), 16), columns_]
                for i in (0, 1)
                for b in range(8)
            ]
            return jnp.dot(pickers[pair], jnp.concatenate(parts, axis=0), preferred_element_type=jnp.float32)

        def columns(q, carry):
            stage[buffer, :, pl.ds(pl.multiple_of(q * SUB, SUB), SUB)] = piece_rows(
                q, data_of(pair)
            ).astype(jnp.bfloat16)
            return carry

        lax.fori_loop(0, QS, columns, 0)
        stored(pair).start()

    def make_pickers():
        lane = lax.broadcasted_iota(jnp.int32, (HD, HD), 1)
        none = jnp.zeros((HD, HD), jnp.float32)
        for pair in range(PAIRS):
            first = jnp.where(lane == turned[:, 2 * pair : 2 * pair + 1], 1.0, 0.0)
            second = jnp.where(lane == turned[:, 2 * pair + 1 : 2 * pair + 2], 1.0, 0.0)
            pickers[pair] = jnp.concatenate(
                [jnp.concatenate([first, none], axis=1), jnp.concatenate([none, second], axis=1)], axis=0
            ).astype(jnp.bfloat16)

    def place_scales():
        lane = lax.broadcasted_iota(jnp.int32, (8, 128), 1)
        parts = [slab[pl.ds(b * 256 + i * 16, 16), pl.ds(SCALES, 128)] for i in (0, 1) for b in range(8)]
        tiles = jnp.concatenate(parts, axis=0)
        for pair in range(PAIRS):
            column = jnp.dot(pickers[pair], tiles, preferred_element_type=jnp.float32)
            chosen = jnp.where(lane == pair, 1.0, 0.0).astype(jnp.bfloat16)
            scale_rows[pl.ds(pair * 8, 8), :] = lax.dot_general(
                chosen,
                column.astype(jnp.bfloat16),
                (((1,), (1,)), ((), ())),
                preferred_element_type=jnp.float32,
            )

    def early_load(k):
        source = tokens if k == 0 else all_tokens.at[place_of(*EARLY[k])]
        return pltpu.make_async_copy(source, held.at[pl.ds(k * ROWS, ROWS)], e_sem.at[k])

    def load_early(low, high):
        for k in range(low, high):
            early_load(k).start()

    def early_out(pair):
        return pltpu.make_async_copy(
            result.at[pair % 2], early.at[:, pl.ds(pair * 256, 256)], o_sem.at[pair % 2]
        )

    def multiply(pair):
        if pair == 0:
            for k in range(len(EARLY)):
                early_load(k).wait()
        if pair >= 2:
            early_out(pair - 2).wait()
        product = lax.dot_general(
            held[...], stage[pair % 2], (((1,), (1,)), ((), ())), preferred_element_type=jnp.float32
        )
        parts = rotated(
            product,
            scale_rows[pl.ds(pair * 8, 1), :],
            cosines_early[...],
            sines_early[...],
            pair == PAIRS - 1,
        )
        for i in (0, 1):
            result[pair % 2, :, pl.ds(i * HD, HD)] = parts[i].astype(jnp.bfloat16)
        early_out(pair).start()

    def stored(pair):
        return pltpu.make_async_copy(
            stage.at[pair % 2], placed.at[pl.ds(pair * 256, 256)], l_sem.at[2 + pair % 2]
        )

    first_sends(0)
    load_rows.wait()

    largest = jnp.zeros((HEADS, 1), jnp.float32)
    for q in range(QS):
        part = jnp.abs(rows[:, pl.ds(q * SUB, SUB)].astype(jnp.float32))
        largest = jnp.maximum(largest, jnp.max(part, axis=1, keepdims=True))
    row_scale = (largest + epsilon).astype(jnp.bfloat16)
    scale = row_scale.astype(jnp.float32)
    for q in range(QS):
        stacked[pl.ds(q * HEADS, HEADS), :] = (
            rows[:, pl.ds(q * SUB, SUB)].astype(jnp.float32) / scale
        ).astype(jnp.bfloat16)
    wide_scale = jnp.broadcast_to(scale, (HEADS, 128)).astype(jnp.bfloat16)

    def head_column(pair):
        row = lax.broadcasted_iota(jnp.int32, (256, 128), 0)
        lane = lax.broadcasted_iota(jnp.int32, (256, 128), 1)
        u, i = row // 16, row % 2
        if pair < 4:
            chosen = jnp.where(lane == u * 8 + 2 * pair + i, query_row[0:1, :], 0)
            return jnp.sum(chosen.astype(jnp.float32), axis=1, keepdims=True).astype(jnp.int32)
        row = lax.broadcasted_iota(jnp.int32, (256, 16), 0)
        lane = lax.broadcasted_iota(jnp.int32, (256, 16), 1)
        chosen = jnp.where(lane == row // 16, kv_row[0:1, :] + QH + KVH * (row % 2), 0)
        return jnp.sum(chosen.astype(jnp.float32), axis=1, keepdims=True).astype(jnp.int32)

    heads = [head_column(pair) for pair in range(PAIRS)]
    def prepare(pair):
        piece_of = (lax.broadcasted_iota(jnp.int32, (256, 1), 0) // 2) % QS
        want = heads[pair] + piece_of * HEADS
        lanes = lax.broadcasted_iota(jnp.int32, (256, QS * HEADS), 1)
        pick = jnp.where(lanes == want, 1.0, 0.0).astype(jnp.bfloat16)
        sending[:, data_of(pair)] = jnp.dot(
            pick, stacked[...], preferred_element_type=jnp.float32
        ).astype(jnp.bfloat16)

    prepare(0)
    scatter(0)
    first_sends(1)
    tile = jnp.zeros((256, 128), jnp.float32)
    lane = lax.broadcasted_iota(jnp.int32, (256, HEADS), 1)
    lane128 = lax.broadcasted_iota(jnp.int32, (256, 128), 1)
    for pair in range(PAIRS):
        pick = jnp.where(lane == heads[pair], 1.0, 0.0).astype(jnp.bfloat16)
        got = jnp.dot(pick, wide_scale, preferred_element_type=jnp.float32)
        tile = jnp.where(lane128 == pair, got, tile)
    sending[:, pl.ds(SCALES, 128)] = tile.astype(jnp.bfloat16)

    prepare(1)
    scatter(1)
    prepare(2)
    scatter(2)
    prepare(3)
    scatter(3)
    prepare(4)
    scatter(4)
    token_step(0)

    turned[...] = jnp.zeros_like(turned)
    for i in range(GROUP):
        if i < 8:
            head = query_s[tp * 8 + i]
        else:
            head = kv_s[tp] + QH + KVH * (i - 8)
        slot = slots[pl.ds(head, 1), :]
        source = ((slot.astype(jnp.float32) + 0.5) * (1.0 / HEADS)).astype(jnp.int32)
        at = ((source // 16) % 2 * 4 + source // 32) * 16 + source % 16
        turned[i : i + 1, :] = at
    turned[...] = jnp.transpose(turned[...].astype(jnp.float32)).astype(jnp.int32)

    def angles():
        lines = jnp.concatenate(
            [position_rows[...].astype(jnp.float32), jnp.zeros((HD - 8, HD), jnp.float32)], axis=0
        )
        lines = jnp.transpose(lines)
        sign = jnp.where(lax.broadcasted_iota(jnp.int32, (HD, HD), 1) < HD // 2, -1.0, 1.0)
        for k in range(8):
            angle = lines[:, k : k + 1] * frequency[0:1, :]
            cosines[pl.ds(k * HD, HD), :] = jnp.cos(angle)
            sines[pl.ds(k * HD, HD), :] = jnp.sin(angle) * sign
        for blocks, c_ref, s_ref in (
            (EARLY, cosines_early, sines_early),
            (LATE, cosines_late, sines_late),
        ):
            for k, offset in enumerate(blocks):
                there = pl.ds(pl.multiple_of(place_of(*offset) * ROWS, ROWS), ROWS)
                c_ref[pl.ds(k * ROWS, ROWS), :] = cosines[there, :]
                s_ref[pl.ds(k * ROWS, ROWS), :] = sines[there, :]

    make_pickers()
    token_step(1)
    token_step(2)
    gathered(0)
    gathered(1)
    gathered(2)
    relayed(0)
    gathered(3)
    angles()
    relayed(1)
    gathered(4)
    relayed(2)
    token_step(4)
    opposite(0)
    crossed(0)
    place(0)
    relayed(3)
    token_step(3)
    token_step(5)
    opposite(1)
    crossed(1)
    place(1)
    place_scales()
    token_step(6)
    load_early(0,9)
    relayed(4)
    multiply(0)
    multiply(1)
    token_step(8)
    opposite(2)
    crossed(2)
    place(2)
    token_step(7)
    opposite(3)
    multiply(2)
    crossed(3)
    place(3)
    opposite(4)
    multiply(3)
    crossed(4)
    place(4)
    multiply(4)
    token_step(9)
    token_step(10)
    token_step(11)

    stored(3).wait()
    stored(4).wait()
    early_out(3).wait()
    early_out(4).wait()
    for copy in started:
        copy.wait_send()
    for pair in range(PAIRS):
        fifteen = sending.at[pl.ds(0, 240), columns_of(pair)]
        pltpu.make_async_copy(fifteen, fifteen, a_send.at[pair]).wait()


def project(
    tokens, placed, scale_rows, early, cosines, sines, refit, out, held, weight, t_sem, w_sem, r_sem
):
    pair = pl.program_id(0)
    tp = lax.axis_index("tp")
    x, z = tp // 4, tp % 4

    def load(k):
        return pltpu.make_async_copy(
            tokens.at[place_at(x, z, *LATE[k])], held.at[pl.ds(k * ROWS, ROWS)], t_sem.at[k]
        )

    def fetch(p):
        return pltpu.make_async_copy(placed.at[pl.ds(p * 256, 256)], weight.at[p], w_sem.at[p])

    def keep(p):
        there = refit.at[pl.ds(pl.multiple_of(p * 256, 256), 256)]
        return pltpu.make_async_copy(weight.at[p], there, r_sem.at[p])

    @pl.when(pair == 0)
    def _():
        fetch(0).start()
        for k in range(len(LATE)):
            load(k).start()
        for p in range(1, PAIRS):
            fetch(p).start()

    there = weight.at[pair]
    pltpu.make_async_copy(there, there, w_sem.at[pair]).wait()
    keep(pair).start()

    def rows_at(offset):
        return pl.ds(pl.multiple_of(place_at(x, z, *offset) * ROWS, ROWS), ROWS)

    for k, offset in enumerate(EARLY):
        out[rows_at(offset), :] = early[pl.ds(k * ROWS, ROWS), :]

    @pl.when(pair == 0)
    def _():
        for k in range(len(LATE)):
            load(k).wait()

    product = lax.dot_general(
        held[...], weight[pair], (((1,), (1,)), ((), ())), preferred_element_type=jnp.float32
    )
    parts = rotated(product, scale_rows[0:1, :], cosines[...], sines[...], pair == PAIRS - 1)
    for i in (0, 1):
        part = parts[i].astype(jnp.bfloat16)
        for k, offset in enumerate(LATE):
            out[rows_at(offset), pl.ds(i * HD, HD)] = part[k * ROWS : (k + 1) * ROWS]

    @pl.when(pair == PAIRS - 1)
    def _():
        for p in range(PAIRS):
            keep(p).wait()


def per_device(learner_rows, learner_slot, query_order, kv_order, tokens, positions):
    any_space = pl.BlockSpec(memory_space=pl.ANY)
    vmem = pl.BlockSpec(memory_space=pltpu.VMEM)
    smem = pl.BlockSpec(memory_space=pltpu.SMEM)
    dma = pltpu.SemaphoreType.DMA
    steps = np.arange(HD // 2, dtype=np.float32) * np.float32(-2.0 * math.log(rope_base) / HD)
    frequency = np.exp(steps).astype(np.float32)
    all_tokens, placed, scale_rows, early, cosines, sines = pl.pallas_call(
        exchange,
        out_shape=(
            jax.ShapeDtypeStruct((16, ROWS, DW), jnp.bfloat16),
            jax.ShapeDtypeStruct((GROUP * HD, DW), jnp.bfloat16),
            jax.ShapeDtypeStruct((PAIRS * 8, 256), jnp.float32),
            jax.ShapeDtypeStruct((E_ROWS, GROUP * HD), jnp.bfloat16),
            jax.ShapeDtypeStruct((L_ROWS, HD), jnp.float32),
            jax.ShapeDtypeStruct((L_ROWS, HD), jnp.float32),
        ),
        in_specs=[any_space, any_space, vmem, vmem, vmem, smem, smem, vmem, vmem],
        out_specs=(any_space, any_space, vmem, any_space, vmem, vmem),
        scratch_shapes=[
            pltpu.VMEM((HEADS, DW), jnp.bfloat16),
            pltpu.VMEM((QS * HEADS, SUB), jnp.bfloat16),
            pltpu.VMEM((256, WIDE), jnp.bfloat16),
            pltpu.VMEM((256, WIDE), jnp.bfloat16),
            pltpu.VMEM((SLOTS, WIDE), jnp.bfloat16),
            pltpu.VMEM((2, 256, DW), jnp.bfloat16),
            pltpu.VMEM((HD, HD), jnp.int32),
            pltpu.VMEM((PAIRS, 256, 256), jnp.bfloat16),
            pltpu.VMEM((SPAN, HD), jnp.float32),
            pltpu.VMEM((SPAN, HD), jnp.float32),
            pltpu.VMEM((E_ROWS, HD), jnp.float32),
            pltpu.VMEM((E_ROWS, HD), jnp.float32),
            pltpu.VMEM((E_ROWS, DW), jnp.bfloat16),
            pltpu.VMEM((2, E_ROWS, 256), jnp.bfloat16),
            dma((44,)),
            dma((44,)),
            dma((40,)),
            dma((20,)),
            dma((PAIRS,)),
            dma((PAIRS,)),
            dma((PAIRS,)),
            dma((4,)),
            dma((PAIRS,)),
            dma((len(EARLY),)),
            dma((2,)),
        ],
        compiler_params=pltpu.CompilerParams(
            collective_id=0, has_side_effects=True, vmem_limit_bytes=62 * 2**20
        ),
    )(
        tokens,
        learner_rows,
        learner_slot.reshape(HEADS, HD),
        query_order.reshape(1, QH),
        kv_order.reshape(1, 16),
        query_order,
        kv_order,
        positions.reshape(8, HD),
        jnp.asarray(np.concatenate([frequency, frequency]).reshape(1, HD)),
    )

    return pl.pallas_call(
        project,
        grid=(PAIRS,),
        out_shape=(
            jax.ShapeDtypeStruct((GROUP * HD, DW), jnp.bfloat16),
            jax.ShapeDtypeStruct((SPAN, GROUP * HD), jnp.bfloat16),
        ),
        in_specs=[
            any_space,
            any_space,
            pl.BlockSpec((8, 256), lambda p: (p, 0)),
            pl.BlockSpec((E_ROWS, 256), lambda p: (0, p)),
            pl.BlockSpec((L_ROWS, HD), lambda p: (0, 0)),
            pl.BlockSpec((L_ROWS, HD), lambda p: (0, 0)),
        ],
        out_specs=(any_space, pl.BlockSpec((SPAN, 256), lambda p: (0, p))),
        scratch_shapes=[
            pltpu.VMEM((L_ROWS, DW), jnp.bfloat16),
            pltpu.VMEM((PAIRS, 256, DW), jnp.bfloat16),
            dma((len(LATE),)),
            dma((PAIRS,)),
            dma((PAIRS,)),
        ],
        compiler_params=pltpu.CompilerParams(vmem_limit_bytes=62 * 2**20),
    )(all_tokens, placed, scale_rows, early, cosines, sines)


def solution(mesh):
    in_specs = (P(("rep", "tp"), None), P(), P(), P(), P(("rep", "tp"), None), P("rep"))
    out_specs = (P("tp", None), P("rep", "tp"))
    return jax.shard_map(
        per_device, mesh=mesh, in_specs=in_specs, out_specs=out_specs, check_vma=False
    )
```
